128 devices in a mesh: batch: 16 (over x, z), proto: 8 (over y, core).
Axes of the slice: x: 4, y: 4, z: 4, core: 2. Of those that a mesh axis runs over, the one named last changes fastest.
Arguments:
- student_feats: bfloat16 [8192, 256], P('batch'), may hold values from -4 to 9
- teacher_feats: bfloat16 [8192, 256], P('batch'), may hold values from -3 to 3
- protos: bfloat16 [256, 65536], P(None, 'proto'), may hold values from -1 to 4
- teacher_protos: bfloat16 [256, 65536], P(None, 'proto'), may hold values from -3 to 3
Outputs:
- grad_feats: float32 [8192, 256], P('batch')
- grad_protos: float32 [256, 65536], P('batch', 'proto')
The draws below stay inside these ranges and needn't reach their ends.
All inputs are finite; a program needn't handle non-finite values.
Results may differ from the reference program's by a relative error of at most 0.0064.
Values sent between devices are 32-bit elements; how exact they have to be, the bound alone decides.
No kernel may reach another device: no remote copies, remote signals or barrier semaphores. Data moves between devices by JAX's collectives and lax.ppermute only.
A program may use at most 128 MiB of HBM per device.

```python
import jax
import jax.numpy as jnp
from jax import lax

K = 256
P_SIZE = 65536
ITERS = 3
B = 8192


def shared_centers(key):
    return jax.random.truncated_normal(key, -4.0, 4.0, (64, K), jnp.float32)


def draw_teacher_feats(key, part):
    centers = shared_centers(key)
    key = jax.random.fold_in(key, 3)
    label_key, scale_key, jitter_key = jax.random.split(key, 3)
    rotation = jax.random.randint(label_key, (), 0, 64)
    labels = (jnp.arange(B, dtype=jnp.int32) * 64 // B + rotation) % 64
    strength = jax.random.uniform(scale_key, (B, 1), jnp.float32, 0.6, 1.4)
    jitter = jax.random.truncated_normal(jitter_key, -4.0, 4.0, (B, K), jnp.float32)
    values = strength * jnp.take(centers, labels, axis=0) + jitter
    return jnp.clip(values, -3.0, 3.0).astype(jnp.bfloat16)


def draw_teacher_protos(key, part):
    centers = shared_centers(key)
    key = jax.random.fold_in(key, 7)
    first_key, second_key, scale_key, jitter_key = jax.random.split(key, 4)
    labels = jnp.minimum(jax.random.randint(first_key, (P_SIZE,), 0, 64), jax.random.randint(second_key, (P_SIZE,), 0, 64))
    strength = jax.random.uniform(scale_key, (1, P_SIZE), jnp.float32, 0.15, 0.45)
    jitter = jax.random.truncated_normal(jitter_key, -4.0, 4.0, (K, P_SIZE), jnp.float32)
    values = strength * jnp.take(centers, labels, axis=0).T + jitter
    return jnp.clip(values, -3.0, 3.0).astype(jnp.bfloat16)


def draw_student_feats(key, part):
    key = jax.random.fold_in(key, 11)
    jitter = jax.random.truncated_normal(key, -4.0, 4.0, (B, K), jnp.float32)
    offset = 4.0
    first = (jnp.arange(K)[None, :] == 0).astype(jnp.float32)
    return (jitter + offset * first).astype(jnp.bfloat16)


def draw_protos(key, part):
    key = jax.random.fold_in(key, 13)
    jitter_key, factor_key = jax.random.split(key, 2)
    jitter = jax.random.truncated_normal(jitter_key, -4.0, 4.0, (K, P_SIZE), jnp.float32) / jnp.sqrt(jnp.float32(K))
    reach = 2.0
    factor = jax.random.uniform(factor_key, (1, P_SIZE), jnp.float32, 0.8, 1.2)
    rising = reach * (jnp.arange(P_SIZE)[None, :].astype(jnp.float32) / P_SIZE) * factor
    first = (jnp.arange(K)[:, None] == 0).astype(jnp.float32)
    return (jitter + rising * first).astype(jnp.bfloat16)


def setup_inputs(seed: int = 0) -> dict:
    arg_keys = jax.random.split(jax.random.key(seed), 5)
    student_feats = draw_student_feats(jax.random.fold_in(arg_keys[4], 71), 0)
    teacher_feats = draw_teacher_feats(jax.random.fold_in(arg_keys[4], 71), 0)
    protos = draw_protos(jax.random.fold_in(arg_keys[4], 71), 0)
    teacher_protos = draw_teacher_protos(jax.random.fold_in(arg_keys[4], 71), 0)
    return {"student_feats": student_feats, "teacher_feats": teacher_feats, "protos": protos, "teacher_protos": teacher_protos}


EPSILON = 1e-06
TEACHER_TEMP = 0.04
STUDENT_TEMP = 0.1

def unit_rows(values):
    wide = values.astype(jnp.float32)
    norms = jnp.sqrt(lax.optimization_barrier(jnp.sum(wide * wide, axis=1, keepdims=True)) + EPSILON)
    return ((wide / norms).astype(jnp.bfloat16), norms)

def unit_columns(values):
    wide = values.astype(jnp.float32)
    norms = jnp.sqrt(lax.optimization_barrier(jnp.sum(wide * wide, axis=0, keepdims=True)) + EPSILON)
    return ((wide / norms).astype(jnp.bfloat16), norms)

def reference(student_feats, teacher_feats, protos, teacher_protos):
    total_rows = student_feats.shape[0]
    width = protos.shape[0]
    total_protos = protos.shape[1]
    teach_z, unused_one = unit_rows(teacher_feats)
    teach_w, unused_two = unit_columns(teacher_protos)
    student_z, student_norm = unit_rows(student_feats)
    student_w, proto_norm = unit_columns(protos)
    block_size = min(total_protos, 4096)
    blocks = total_protos // block_size
    teach_blocks = teach_w.reshape(width, blocks, block_size).transpose(1, 0, 2)
    student_blocks = student_w.reshape(width, blocks, block_size).transpose(1, 0, 2)

    def energy_of(wblock):
        return jnp.exp(jnp.dot(teach_z, wblock, preferred_element_type=jnp.float32) / TEACHER_TEMP)
    col_scale = jnp.ones((blocks, block_size), jnp.float32)
    row_scale = jnp.ones((total_rows,), jnp.float32)
    for step_index in range(ITERS):

        def col_pass(pair):
            wblock, scale_block = pair
            return scale_block * lax.optimization_barrier(jnp.sum(energy_of(wblock) * row_scale[:, None], axis=0))
        col_total = lax.map(col_pass, (teach_blocks, col_scale))
        col_scale = col_scale / (total_protos * col_total)

        def row_pass(carry, pair):
            wblock, scale_block = pair
            return (carry + lax.optimization_barrier(jnp.sum(energy_of(wblock) * scale_block[None, :], axis=1)), None)
        row_acc, unused = lax.scan(row_pass, jnp.zeros((total_rows,), jnp.float32), (teach_blocks, col_scale))
        row_total = row_scale * row_acc
        row_scale = row_scale / (total_rows * row_total)

    def soft_pass(carry, wblock):
        raw = jnp.dot(student_z, wblock, preferred_element_type=jnp.float32)
        return (carry + lax.optimization_barrier(jnp.sum(jnp.exp(raw / STUDENT_TEMP), axis=1)), None)
    totals, unused = lax.scan(soft_pass, jnp.zeros((total_rows,), jnp.float32), student_blocks)

    def grad_pass(carry, triple):
        wblock, tblock, scale_block = triple
        raw = jnp.dot(student_z, wblock, preferred_element_type=jnp.float32)
        prob = jnp.exp(raw / STUDENT_TEMP) / totals[:, None]
        targets = energy_of(tblock) * scale_block[None, :] * row_scale[:, None] * total_rows
        dscore = ((prob - targets) / STUDENT_TEMP).astype(jnp.bfloat16)
        carry = carry + jnp.dot(dscore, wblock.T, preferred_element_type=jnp.float32)
        gblock = jnp.dot(student_z.T, dscore, preferred_element_type=jnp.float32)
        return (carry, gblock)
    feat_sum, gblocks = lax.scan(grad_pass, jnp.zeros((total_rows, width), jnp.float32), (student_blocks, teach_blocks, col_scale))
    proto_sum = gblocks.transpose(1, 0, 2).reshape(width, total_protos)
    zs_wide = student_z.astype(jnp.float32)
    along = lax.optimization_barrier(jnp.sum(zs_wide * feat_sum, axis=1, keepdims=True))
    grad_feats = (feat_sum - zs_wide * along) / student_norm
    ws_wide = student_w.astype(jnp.float32)
    dots = lax.optimization_barrier(jnp.sum(ws_wide * proto_sum, axis=0, keepdims=True))
    grad_protos = (proto_sum - ws_wide * dots) / proto_norm
    return (grad_feats, grad_protos)
```

```python
import functools

import jax
import jax.numpy as jnp
from jax import lax
from jax.experimental import pallas as pl
from jax.experimental.pallas import tpu as pltpu
from jax.sharding import Mesh
from jax.sharding import PartitionSpec as P

EPSILON = 1e-06
TEACHER_SCALE = 25.0
STUDENT_SCALE = 10.0
LOG2E = 1.4426950408889634
SIZES = {"x": 4, "z": 4, "y": 4, "core": 2}
BATCH = ("x", "z")
PROTO = ("y", "core")
WHOLE = pl.BlockSpec(memory_space=pltpu.VMEM)
F32 = jnp.float32
BF16 = jnp.bfloat16


def params(mib):
    return pltpu.CompilerParams(vmem_limit_bytes=mib << 20)


def in_vmem(value):
    return pltpu.with_memory_space_constraint(value, pltpu.VMEM)


def unit_rows(values):
    wide = values.astype(F32)
    norms = jnp.sqrt(jnp.sum(wide * wide, axis=1, keepdims=True) + EPSILON)
    return (wide / norms).astype(BF16), norms


def unit_columns(values):
    wide = values.astype(F32)
    norms = jnp.sqrt(jnp.sum(wide * wide, axis=0, keepdims=True) + EPSILON)
    return (wide * (1.0 / norms)).astype(BF16), norms


def columns_of(step, size):
    return pl.ds(pl.multiple_of(step * size, size), size)


def across(row, lanes=128):
    return jnp.broadcast_to(row, (lanes, row.shape[1])).T


def two_terms(row):
    high = row.astype(BF16).astype(F32)
    place = lax.broadcasted_iota(jnp.int32, (16, row.shape[1]), 0)
    return jnp.where(place == 0, high, jnp.where(place == 1, row - high, 0.0)).astype(BF16)


def energy_kernel(feats, protos, energy, col_sum, *, size):
    here = columns_of(pl.program_id(0), size)
    unit, _ = unit_columns(protos[...])
    score = jnp.dot(feats[...], unit, preferred_element_type=F32)
    value = jnp.exp2(score * (TEACHER_SCALE * LOG2E))
    energy[:, here] = value.astype(BF16)
    col_sum[:, here] = jnp.sum(value, axis=0, keepdims=True)


def energy_call(feats, protos, size=1024):
    rows, width = feats.shape
    count = protos.shape[1]
    return pl.pallas_call(
        functools.partial(energy_kernel, size=size),
        grid=(count // size,),
        in_specs=[pl.BlockSpec((rows, width), lambda i: (0, 0)), pl.BlockSpec((width, size), lambda i: (0, i))],
        out_specs=[WHOLE, WHOLE],
        out_shape=[pltpu.VMEM((rows, count), BF16), jax.ShapeDtypeStruct((1, count), F32)],
        compiler_params=params(12),
        name="energy",
    )(feats, protos)


def student_kernel(feats, protos, expo, unit_out, norm_out, row_sum, total, *, size):
    step = pl.program_id(0)
    here = columns_of(step, size)
    unit, norm = unit_columns(protos[...])
    unit_out[:, here] = unit
    norm_out[:, here] = norm
    score = jnp.dot(feats[...], unit, preferred_element_type=F32)
    value = jnp.exp2(score * (STUDENT_SCALE * LOG2E))
    expo[:, here] = value.astype(BF16)
    lanes = value[:, :128]
    for tile in range(1, size // 128):
        lanes = lanes + value[:, tile * 128 : (tile + 1) * 128]

    @pl.when(step == 0)
    def _():
        total[...] = lanes

    @pl.when(step > 0)
    def _():
        total[...] += lanes

    @pl.when(step == pl.num_programs(0) - 1)
    def _():
        row_sum[...] = jnp.sum(total[...].T, axis=0, keepdims=True)


def student_call(feats, protos, size=1024):
    rows, width = feats.shape
    count = protos.shape[1]
    return pl.pallas_call(
        functools.partial(student_kernel, size=size),
        grid=(count // size,),
        in_specs=[pl.BlockSpec((rows, width), lambda i: (0, 0)), pl.BlockSpec((width, size), lambda i: (0, i))],
        out_specs=[WHOLE] * 4,
        out_shape=[
            pltpu.VMEM((rows, count), BF16),
            pltpu.VMEM((width, count), BF16),
            jax.ShapeDtypeStruct((1, count), F32),
            jax.ShapeDtypeStruct((1, rows), F32),
        ],
        scratch_shapes=[pltpu.VMEM((rows, 128), F32)],
        compiler_params=params(12),
        name="student",
    )(feats, protos)


def row_kernel(energy, col_total, row_part, *, total_protos, size=1024):
    rows, count = energy.shape
    total = jnp.zeros((16, rows), F32)
    for at in range(0, count, size):
        scale = two_terms(1.0 / (total_protos * col_total[:, at : at + size]))
        total = total + lax.dot_general(
            scale, energy[:, at : at + size], (((1,), (1,)), ((), ())), preferred_element_type=F32
        )
    row_part[...] = jnp.sum(total, axis=0, keepdims=True)


def row_call(energy, col_total, total_protos):
    return pl.pallas_call(
        functools.partial(row_kernel, total_protos=total_protos),
        in_specs=[WHOLE, WHOLE],
        out_specs=WHOLE,
        out_shape=jax.ShapeDtypeStruct((1, energy.shape[0]), F32),
        compiler_params=params(4),
        name="row_pass",
    )(in_vmem(energy), col_total)


def col_kernel(energy, row_total, col_part, *, total_rows, size=1024):
    scale = two_terms(1.0 / (total_rows * row_total[...]))
    for at in range(0, energy.shape[1], size):
        part = jnp.dot(scale, energy[:, at : at + size], preferred_element_type=F32)
        col_part[:, at : at + size] = jnp.sum(part, axis=0, keepdims=True)


def col_call(energy, row_total, total_rows):
    return pl.pallas_call(
        functools.partial(col_kernel, total_rows=total_rows),
        in_specs=[WHOLE, WHOLE],
        out_specs=WHOLE,
        out_shape=jax.ShapeDtypeStruct((1, energy.shape[1]), F32),
        compiler_params=params(4),
        name="col_pass",
    )(in_vmem(energy), row_total)


def grad_kernel(
    energy, expo, feats, unit, norm, col_total, row_total, soft_total, feat_part, grad, row_scale, soft_scale,
    *, total_protos, size,
):
    step = pl.program_id(0)
    here = columns_of(step, size)

    @pl.when(step == 0)
    def _():
        row_scale[...] = across(STUDENT_SCALE / row_total[...])
        soft_scale[...] = across(STUDENT_SCALE / soft_total[...])

    col_scale = 1.0 / (total_protos * col_total[:, here])
    target = energy[:, here].astype(F32) * col_scale
    prob = expo[:, here].astype(F32)
    wide = size // 128
    rows_r = jnp.concatenate([row_scale[...]] * wide, axis=1)
    rows_s = jnp.concatenate([soft_scale[...]] * wide, axis=1)
    dscore = (prob * rows_s - target * rows_r).astype(BF16)
    weights = unit[:, here]
    part = lax.dot_general(dscore, weights, (((1,), (1,)), ((), ())), preferred_element_type=F32)

    @pl.when(step == 0)
    def _():
        feat_part[...] = part

    @pl.when(step > 0)
    def _():
        feat_part[...] += part

    proto_part = lax.dot_general(feats[...], dscore, (((0,), (0,)), ((), ())), preferred_element_type=F32)
    wide_unit = weights.astype(F32)
    dots = jnp.sum(wide_unit * proto_part, axis=0, keepdims=True)
    grad[...] = (proto_part - wide_unit * dots) * (1.0 / norm[:, here])


def grad_call(energy, expo, feats, unit, norm, col_total, row_total, soft_total, total_protos, size=1024):
    rows, count = energy.shape
    width = unit.shape[0]
    return pl.pallas_call(
        functools.partial(grad_kernel, total_protos=total_protos, size=size),
        grid=(count // size,),
        in_specs=[WHOLE] * 8,
        out_specs=[WHOLE, pl.BlockSpec((width, size), lambda i: (0, i))],
        out_shape=[jax.ShapeDtypeStruct((rows, width), F32), jax.ShapeDtypeStruct((width, count), F32)],
        scratch_shapes=[pltpu.VMEM((rows, 128), F32)] * 2,
        compiler_params=params(16),
        name="grad",
    )(in_vmem(energy), in_vmem(expo), feats, in_vmem(unit), norm, col_total, row_total, soft_total)


def shifted(value, axis, shift):
    size = SIZES[axis]
    return lax.ppermute(value, axis, [(i, (i + shift) % size) for i in range(size)])


def ring_sum(value, axis):
    parts = [shifted(value, axis, shift) for shift in ((1, 3, 2) if SIZES[axis] == 4 else (1,))]
    for part in parts:
        value = value + part
    return value


def summed(value, axes):
    for axis in axes:
        value = ring_sum(value, axis)
    return value


def on_device(student_feats, teacher_feats, protos, teacher_protos):
    rows = student_feats.shape[0]
    total_rows = rows * 16
    total_protos = protos.shape[1] * 8
    teacher_unit, _ = unit_rows(teacher_feats)
    student_unit, student_norm = unit_rows(student_feats)
    energy, col_part = energy_call(teacher_unit, teacher_protos)
    col_total = summed(col_part, BATCH)
    expo, unit, norm, soft_part = student_call(student_unit, protos)
    row_part = row_call(energy, col_total, total_protos)
    both = summed(jnp.concatenate([row_part, soft_part], axis=0), ("core", "y"))
    row_total, soft_total = both[:1], both[1:]
    for _ in range(2):
        col_total = summed(col_call(energy, row_total, total_rows), BATCH)
        row_total = summed(row_call(energy, col_total, total_protos), ("core", "y"))
    feat_part, grad_part = grad_call(
        energy, expo, student_unit, unit, norm, col_total, row_total, soft_total, total_protos
    )
    grad_protos = lax.psum_scatter(grad_part, BATCH, scatter_dimension=0, tiled=True)

    core = lax.axis_index("core")
    half = rows // 2
    mine = lax.dynamic_slice_in_dim(feat_part, core * half, half, 0)
    other = lax.dynamic_slice_in_dim(feat_part, (1 - core) * half, half, 0)
    feat_sum = ring_sum(mine + shifted(other, "core", 1), "y")
    unit_here = lax.dynamic_slice_in_dim(student_unit, core * half, half, 0).astype(F32)
    norm_here = lax.dynamic_slice_in_dim(student_norm, core * half, half, 0)
    along = jnp.sum(unit_here * feat_sum, axis=1, keepdims=True)
    grad_here = (feat_sum - unit_here * along) / norm_here
    grad_there = shifted(grad_here, "core", 1)
    first = jnp.where(core == 0, grad_here, grad_there)
    second = jnp.where(core == 0, grad_there, grad_here)
    return jnp.concatenate([first, second], axis=0), grad_protos


def solution(mesh):
    split = Mesh(mesh.devices.reshape(4, 4, 4, 2), ("x", "z", "y", "core"))
    return jax.shard_map(
        on_device,
        mesh=split,
        in_specs=(P(BATCH, None), P(BATCH, None), P(None, PROTO), P(None, PROTO)),
        out_specs=(P(BATCH, None), P(BATCH, PROTO)),
        check_vma=False,
    )
```

```python
import functools

import jax
import jax.numpy as jnp
from jax import lax
from jax.experimental import pallas as pl
from jax.experimental.pallas import tpu as pltpu
from jax.sharding import Mesh
from jax.sharding import PartitionSpec as P

EPSILON = 1e-06
TEACHER_SCALE = 25.0
STUDENT_SCALE = 10.0
LOG2E = 1.4426950408889634
SIZES = {"x": 4, "z": 4, "y": 4, "core": 2}
BATCH = ("x", "z")
PROTO = ("y", "core")
WHOLE = pl.BlockSpec(memory_space=pltpu.VMEM)
SCALARS = pl.BlockSpec(memory_space=pltpu.SMEM)
ANY = pl.BlockSpec(memory_space=pl.ANY)
F32 = jnp.float32
BF16 = jnp.bfloat16


def params(mib):
    return pltpu.CompilerParams(vmem_limit_bytes=mib << 20)


def cost(microseconds):
    return pl.CostEstimate(flops=0, bytes_accessed=int(microseconds * 3.0e6), transcendentals=0)


def in_vmem(value):
    return pltpu.with_memory_space_constraint(value, pltpu.VMEM)


def in_hbm(value):
    return pltpu.with_memory_space_constraint(value, pltpu.HBM)


def unit_rows(values):
    wide = values.astype(F32)
    norms = jnp.sqrt(jnp.sum(wide * wide, axis=1, keepdims=True) + EPSILON)
    return (wide / norms).astype(BF16), norms


def unit_columns(values):
    wide = values.astype(F32)
    norms = jnp.sqrt(jnp.sum(wide * wide, axis=0, keepdims=True) + EPSILON)
    return (wide * (1.0 / norms)).astype(BF16), norms


def across(row, lanes=128):
    return jnp.broadcast_to(row, (lanes, row.shape[1])).T


def two_terms(row):
    high = row.astype(BF16).astype(F32)
    place = lax.broadcasted_iota(jnp.int32, (16, row.shape[1]), 0)
    return jnp.where(place == 0, high, jnp.where(place == 1, row - high, 0.0)).astype(BF16)


def fetch(source, held, arrived, chunk, start=0):
    copies = [
        pltpu.make_async_copy(
            source.at[:, pl.ds(start + at, chunk)], held.at[:, at : at + chunk], arrived.at[at // chunk]
        )
        for at in range(0, held.shape[1], chunk)
    ]
    for copy in copies:
        copy.start()
    return copies


def energy_kernel(place, feats, protos, energy, col_sum, held, arrived, *, size, chunk):
    copies = fetch(protos, held, arrived, chunk)
    teacher, _ = unit_rows(feats[...])
    for at in range(0, held.shape[1], size):
        if at % chunk == 0:
            copies[at // chunk].wait()
        unit, _ = unit_columns(held[:, at : at + size])
        score = jnp.dot(teacher, unit, preferred_element_type=F32)
        value = jnp.exp2(score * (TEACHER_SCALE * LOG2E))
        energy[:, at : at + size] = value.astype(BF16)
        col_sum[:, at : at + size] = jnp.sum(value, axis=0, keepdims=True)


def energy_call(place, feats, protos, size=512, chunk=2048):
    rows, width = feats.shape
    count = protos.shape[1]
    return pl.pallas_call(
        functools.partial(energy_kernel, size=size, chunk=chunk),
        in_specs=[SCALARS, WHOLE, ANY],
        out_specs=[WHOLE, WHOLE],
        out_shape=[pltpu.VMEM((rows, count), BF16), jax.ShapeDtypeStruct((1, count), F32)],
        scratch_shapes=[pltpu.VMEM((width, count), BF16), pltpu.SemaphoreType.DMA((count // chunk,))],
        compiler_params=params(16),
        cost_estimate=cost(5.0),
        name="energy",
    )(place, in_hbm(feats), in_hbm(protos))


def units_kernel(place, teacher, student, both):
    rows, width = both.shape
    here = pl.ds(pl.multiple_of(place[1] * rows, rows), rows)
    both[:, : width // 2] = unit_rows(teacher[here, :])[0].astype(F32)
    both[:, width // 2 :] = unit_rows(student[here, :])[0].astype(F32)


def units_call(place, teacher, student):
    rows, width = teacher.shape
    return pl.pallas_call(
        units_kernel,
        in_specs=[SCALARS, WHOLE, WHOLE],
        out_specs=WHOLE,
        out_shape=jax.ShapeDtypeStruct((rows // 2, 2 * width), F32),
        compiler_params=params(8),
        cost_estimate=cost(1.5),
        name="units",
    )(place, in_hbm(teacher), in_hbm(student))


def student_kernel(feats, protos, *refs, size, chunk):
    expo, unit_out, row_sum, held, arrived = refs[-5:]
    copies = fetch(protos, held, arrived, chunk)
    student, _ = unit_rows(feats[...])
    total = jnp.zeros((feats.shape[0], 128), F32)
    for at in range(0, held.shape[1], size):
        if at % chunk == 0:
            copies[at // chunk].wait()
        unit, _ = unit_columns(held[:, at : at + size])
        unit_out[:, at : at + size] = unit
        score = jnp.dot(student, unit, preferred_element_type=F32)
        value = jnp.exp2(score * (STUDENT_SCALE * LOG2E))
        expo[:, at : at + size] = value.astype(BF16)
        for tile in range(0, size, 128):
            total = total + value[:, tile : tile + 128]
    row_sum[...] = jnp.sum(total.T, axis=0, keepdims=True)


def student_call(feats, protos, after=(), size=512, chunk=2048):
    rows, width = feats.shape
    count = protos.shape[1]
    return pl.pallas_call(
        functools.partial(student_kernel, size=size, chunk=chunk),
        in_specs=[WHOLE, ANY] + [ANY] * len(after),
        out_specs=[WHOLE] * 3,
        out_shape=[
            pltpu.VMEM((rows, count), BF16),
            pltpu.VMEM((width, count), BF16),
            jax.ShapeDtypeStruct((1, rows), F32),
        ],
        scratch_shapes=[pltpu.VMEM((width, count), BF16), pltpu.SemaphoreType.DMA((count // chunk,))],
        compiler_params=params(16),
        cost_estimate=cost(6.0),
        name="student",
    )(in_hbm(feats), in_hbm(protos), *after)


def tall_kernel(place, protos, *refs, pieces, turn, scale, size=512):
    energy = refs[len(refs) - 3 - turn]
    held, arrived = refs[-2:]
    rows = refs[0].shape[0]
    width, count = held.shape
    (copy,) = fetch(protos, held, arrived, count, pl.multiple_of(place[0] * count, count))
    side = slice(width, 2 * width) if turn else slice(0, width)
    feats = [refs[k][:, side] for k in range(pieces)]
    if turn:
        turned = refs[-3]
        for k in range(pieces):
            turned[:, k * rows : (k + 1) * rows] = feats[k].T.astype(BF16)
    feats = [value.astype(BF16) for value in feats]
    copy.wait()
    for at in range(0, count, size):
        unit, _ = unit_columns(held[:, at : at + size])
        for k in range(pieces):
            score = jnp.dot(feats[k], unit, preferred_element_type=F32)
            energy[k * rows : (k + 1) * rows, at : at + size] = jnp.exp2(score * (scale * LOG2E)).astype(BF16)


def tall_call(place, protos, feats, turn, scale, name, after=()):
    rows = feats[0].shape[0] * len(feats)
    width, count = protos.shape
    count = count // 4
    out_shape = [pltpu.VMEM((rows, count), BF16)]
    if turn:
        out_shape.append(jax.ShapeDtypeStruct((width, rows), BF16))
    return pl.pallas_call(
        functools.partial(tall_kernel, pieces=len(feats), turn=turn, scale=scale),
        in_specs=[SCALARS, ANY] + [WHOLE] * len(feats) + [ANY] * len(after),
        out_specs=[WHOLE] * len(out_shape),
        out_shape=out_shape,
        scratch_shapes=[pltpu.VMEM((width, count), BF16), pltpu.SemaphoreType.DMA((1,))],
        compiler_params=params(16),
        cost_estimate=cost(5.0),
        name=name,
    )(place, in_hbm(protos), *feats, *after)


def row_kernel(energy, col_total, *refs, total_protos, size=1024):
    row_part = refs[-1]
    rows, count = energy.shape
    total = jnp.zeros((16, rows), F32)
    for at in range(0, count, size):
        scale = two_terms(1.0 / (total_protos * col_total[:, at : at + size]))
        total = total + lax.dot_general(
            scale, energy[:, at : at + size], (((1,), (1,)), ((), ())), preferred_element_type=F32
        )
    row_part[...] = jnp.sum(total, axis=0, keepdims=True)


def row_call(energy, col_total, total_protos, after=()):
    return pl.pallas_call(
        functools.partial(row_kernel, total_protos=total_protos),
        in_specs=[WHOLE, WHOLE] + [ANY] * len(after),
        out_specs=WHOLE,
        out_shape=jax.ShapeDtypeStruct((1, energy.shape[0]), F32),
        compiler_params=params(4),
        name="row_pass",
    )(in_vmem(energy), col_total, *after)


def col_kernel(energy, row_total, *refs, total_rows, size=1024):
    col_part = refs[-1]
    scale = two_terms(1.0 / (total_rows * row_total[...]))
    for at in range(0, energy.shape[1], size):
        part = jnp.dot(scale, energy[:, at : at + size], preferred_element_type=F32)
        col_part[:, at : at + size] = jnp.sum(part, axis=0, keepdims=True)


def col_call(energy, row_total, total_rows, after=()):
    return pl.pallas_call(
        functools.partial(col_kernel, total_rows=total_rows),
        in_specs=[WHOLE, WHOLE] + [ANY] * len(after),
        out_specs=WHOLE,
        out_shape=jax.ShapeDtypeStruct((1, energy.shape[1]), F32),
        compiler_params=params(4),
        name="col_pass",
    )(in_vmem(energy), row_total, *after)


def scaled_difference(energy, expo, col_total, row_scale, soft_scale, total_protos):
    wide = energy.shape[1] // 128
    rows_r = jnp.concatenate([row_scale[...]] * wide, axis=1)
    rows_s = jnp.concatenate([soft_scale[...]] * wide, axis=1)
    target = energy.astype(F32) * (1.0 / (total_protos * col_total))
    return (expo.astype(F32) * rows_s - target * rows_r).astype(BF16)


def feat_kernel(place, energy, expo, unit, col_total, row_total, soft_total, mine, other, total, row_scale, soft_scale, *, total_protos, size):
    row_scale[...] = across(STUDENT_SCALE / row_total[...])
    soft_scale[...] = across(STUDENT_SCALE / soft_total[...])
    for at in range(0, energy.shape[1], size):
        here = slice(at, at + size)
        dscore = scaled_difference(
            energy[:, here], expo[:, here], col_total[:, here], row_scale, soft_scale, total_protos
        )
        part = lax.dot_general(dscore, unit[:, here], (((1,), (1,)), ((), ())), preferred_element_type=F32)
        if at:
            total[...] += part
        else:
            total[...] = part
    rows = mine.shape[0]
    mine[...] = total[pl.ds(pl.multiple_of(place[1] * rows, rows), rows), :]
    other[...] = total[pl.ds(pl.multiple_of((1 - place[1]) * rows, rows), rows), :]


def feat_call(place, energy, expo, unit, col_total, row_total, soft_total, total_protos, size=1024):
    rows, count = energy.shape
    width = unit.shape[0]
    return pl.pallas_call(
        functools.partial(feat_kernel, total_protos=total_protos, size=size),
        in_specs=[SCALARS] + [WHOLE] * 6,
        out_specs=[WHOLE] * 2,
        out_shape=[jax.ShapeDtypeStruct((rows // 2, width), F32)] * 2,
        scratch_shapes=[pltpu.VMEM((rows, width), F32)] + [pltpu.VMEM((rows, 128), F32)] * 2,
        compiler_params=params(16),
        cost_estimate=cost(6.0),
        name="feat_grad",
    )(place, in_vmem(energy), in_vmem(expo), in_vmem(unit), col_total, row_total, soft_total)


def proto_kernel(place, protos, energy, expo, turned, col_total, *refs, pieces, total_protos, size):
    totals = refs[:pieces]
    grad, held, made, row_scale, soft_scale, arrived, left = refs[-7:]
    width, count = held.shape
    first = pl.multiple_of(place[0] * count, count)
    (copy,) = fetch(protos, held, arrived, count, first)
    rows = energy.shape[0] // pieces // 2
    for k in range(pieces):
        row_wide = across(STUDENT_SCALE / totals[k][:1, :])
        soft_wide = across(STUDENT_SCALE / totals[k][1:, :])
        for half in range(2):
            side = jnp.where(place[1] == half, 0, 1)
            there = pl.ds(pl.multiple_of(side * (pieces * rows) + k * rows, rows), rows)
            row_scale[there, :] = row_wide[half * rows : (half + 1) * rows]
            soft_scale[there, :] = soft_wide[half * rows : (half + 1) * rows]
    copy.wait()
    copies = []
    for at in range(0, count, size):
        here = slice(at, at + size)
        dscore = scaled_difference(
            energy[:, here], expo[:, here], col_total[:, pl.ds(first + at, size)], row_scale, soft_scale, total_protos
        )
        part = jnp.dot(turned[...], dscore, preferred_element_type=F32)
        unit, norm = unit_columns(held[:, here])
        wide_unit = unit.astype(F32)
        dots = jnp.sum(wide_unit * part, axis=0, keepdims=True)
        made[:, here] = (part - wide_unit * dots) * (1.0 / norm)
        copies.append(pltpu.make_async_copy(made.at[:, here], grad.at[:, here], left.at[at // size]))
        copies[-1].start()
    for copy in copies:
        copy.wait()


def proto_call(place, protos, energy, expo, turned, col_total, totals, total_protos, after=(), size=512):
    rows, count = energy.shape
    width = protos.shape[0]
    return pl.pallas_call(
        functools.partial(proto_kernel, pieces=len(totals), total_protos=total_protos, size=size),
        in_specs=[SCALARS, ANY] + [WHOLE] * (4 + len(totals)) + [ANY] * len(after),
        out_specs=ANY,
        out_shape=pltpu.HBM((width, count), F32),
        scratch_shapes=[
            pltpu.VMEM((width, count), BF16),
            pltpu.VMEM((width, count), F32),
            pltpu.VMEM((rows, 128), F32),
            pltpu.VMEM((rows, 128), F32),
            pltpu.SemaphoreType.DMA((1,)),
            pltpu.SemaphoreType.DMA((count // size,)),
        ],
        compiler_params=params(20),
        cost_estimate=cost(8.0),
        name="proto_grad",
    )(place, in_hbm(protos), in_vmem(energy), in_vmem(expo), turned, col_total, *totals, *after)


def finish_kernel(place, feats, first, second, third, fourth, grad):
    rows = grad.shape[0]
    here = pl.ds(pl.multiple_of(place[1] * rows, rows), rows)
    unit, norm = unit_rows(feats[here, :])
    unit = unit.astype(F32)
    feat_sum = (first[...] + second[...]) + (third[...] + fourth[...])
    along = jnp.sum(unit * feat_sum, axis=1, keepdims=True)
    grad[...] = (feat_sum - unit * along) / norm


def finish_call(place, feats, parts):
    return pl.pallas_call(
        finish_kernel,
        in_specs=[SCALARS] + [WHOLE] * (1 + len(parts)),
        out_specs=WHOLE,
        out_shape=jax.ShapeDtypeStruct(parts[0].shape, F32),
        compiler_params=params(8),
        cost_estimate=cost(1.0),
        name="finish",
    )(place, feats, *parts)


def join_kernel(place, mine, other, whole):
    rows = mine.shape[0]
    whole[pl.ds(pl.multiple_of(place[1] * rows, rows), rows), :] = mine[...]
    whole[pl.ds(pl.multiple_of((1 - place[1]) * rows, rows), rows), :] = other[...]


def join_call(place, mine, other):
    rows, width = mine.shape
    return pl.pallas_call(
        join_kernel,
        in_specs=[SCALARS, WHOLE, WHOLE],
        out_specs=WHOLE,
        out_shape=jax.ShapeDtypeStruct((2 * rows, width), F32),
        compiler_params=params(8),
        cost_estimate=cost(1.0),
        name="join",
    )(place, mine, other)


def shifted(value, axis, shift):
    size = SIZES[axis]
    return lax.ppermute(value, axis, [(i, (i + shift) % size) for i in range(size)])


def ring_parts(value, axis):
    shifts = (1, 2, 3) if SIZES[axis] == 4 else (1,)
    return [value] + [shifted(value, axis, shift) for shift in shifts]


def ring_sum(value, axis):
    parts = ring_parts(value, axis)
    value = parts[0]
    for part in parts[1:]:
        value = value + part
    return value


def batch_sum(value):
    return ring_sum(ring_sum(value, "x"), "z")


def proto_sum(value):
    return ring_sum(ring_sum(value, "core"), "y")


def on_device(student_feats, teacher_feats, protos, teacher_protos):
    rows, width = student_feats.shape
    count = protos.shape[1]
    total_rows = rows * 16
    total_protos = count * 8
    place = jnp.stack([lax.axis_index("z"), lax.axis_index("core")]).astype(jnp.int32)

    energy, col_part = energy_call(place, teacher_feats, teacher_protos)
    col_total = batch_sum(col_part)
    tall = ring_parts(units_call(place, teacher_feats, student_feats), "z")
    tall = tall + [shifted(part, "core", 1) for part in tall]
    expo, unit, soft_part = student_call(student_feats, protos, (col_part,))
    row_part = row_call(energy, col_total, total_protos, (soft_part,))
    row_total = proto_sum(row_part)
    col_total = batch_sum(col_call(energy, row_total, total_rows))
    row_part = row_call(energy, col_total, total_protos, (tall[-1],))
    row_total = proto_sum(row_part)
    col_part = col_call(energy, row_total, total_rows)
    col_total = batch_sum(col_part)
    (tall_energy,) = tall_call(place, teacher_protos, tall, 0, TEACHER_SCALE, "tall_energy", (col_part,))
    tall_expo, turned = tall_call(place, protos, tall, 1, STUDENT_SCALE, "tall_expo", (col_part,))
    row_part = row_call(energy, col_total, total_protos, (turned,))
    totals = proto_sum(jnp.concatenate([row_part, soft_part], axis=0))
    mine, other = feat_call(place, energy, expo, unit, col_total, totals[:1], totals[1:], total_protos)
    feat_half = mine + shifted(other, "core", 1)
    grad_part = proto_call(
        place, protos, tall_energy, tall_expo, turned, col_total, ring_parts(totals, "z"), total_protos, (feat_half,)
    )
    pieces = lax.all_to_all(grad_part.reshape(16, width // 16, count // 4), BATCH, 0, 0)
    pieces = jnp.sum(pieces.reshape(4, 4, width // 16, count // 4), axis=0)
    grad_protos = pieces.transpose(1, 0, 2).reshape(width // 16, count)

    grad_half = finish_call(place, student_feats, ring_parts(feat_half, "y"))
    return join_call(place, grad_half, shifted(grad_half, "core", 1)), grad_protos


def solution(mesh):
    split = Mesh(mesh.devices.reshape(4, 4, 4, 2), ("x", "z", "y", "core"))
    return jax.shard_map(
        on_device,
        mesh=split,
        in_specs=(P(BATCH, None), P(BATCH, None), P(None, PROTO), P(None, PROTO)),
        out_specs=(P(BATCH, None), P(BATCH, PROTO)),
        check_vma=False,
    )
```

```python
import functools

import jax
import jax.numpy as jnp
from jax import lax
from jax.experimental import pallas as pl
from jax.experimental.pallas import tpu as pltpu
from jax.sharding import Mesh
from jax.sharding import PartitionSpec as P

EPSILON = 1e-06
TEACHER_SCALE = 25.0
STUDENT_SCALE = 10.0
LOG2E = 1.4426950408889634
SIZES = {"x": 4, "z": 4, "y": 4, "core": 2}
BATCH = ("x", "z")
PROTO = ("y", "core")
WHOLE = pl.BlockSpec(memory_space=pltpu.VMEM)
SCALARS = pl.BlockSpec(memory_space=pltpu.SMEM)
ANY = pl.BlockSpec(memory_space=pl.ANY)
F32 = jnp.float32
BF16 = jnp.bfloat16


def params(mib):
    return pltpu.CompilerParams(vmem_limit_bytes=mib << 20)


def cost(microseconds):
    return pl.CostEstimate(flops=0, bytes_accessed=int(microseconds * 3.0e6), transcendentals=0)


def in_vmem(value):
    return pltpu.with_memory_space_constraint(value, pltpu.VMEM)


def in_hbm(value):
    return pltpu.with_memory_space_constraint(value, pltpu.HBM)


def unit_rows(values):
    wide = values.astype(F32)
    norms = jnp.sqrt(jnp.sum(wide * wide, axis=1, keepdims=True) + EPSILON)
    return (wide / norms).astype(BF16), norms


def unit_columns(values):
    wide = values.astype(F32)
    norms = jnp.sqrt(jnp.sum(wide * wide, axis=0, keepdims=True) + EPSILON)
    return (wide * (1.0 / norms)).astype(BF16), norms


def across(row, lanes=128):
    return jnp.broadcast_to(row, (lanes, row.shape[1])).T


def two_terms(row):
    high = row.astype(BF16).astype(F32)
    place = lax.broadcasted_iota(jnp.int32, (16, row.shape[1]), 0)
    return jnp.where(place == 0, high, jnp.where(place == 1, row - high, 0.0)).astype(BF16)


def fetch(source, held, arrived, chunk, start=0):
    copies = [
        pltpu.make_async_copy(
            source.at[:, pl.ds(start + at, chunk)], held.at[:, at : at + chunk], arrived.at[at // chunk]
        )
        for at in range(0, held.shape[1], chunk)
    ]
    for copy in copies:
        copy.start()
    return copies


def energy_kernel(place, feats, protos, *refs, size, chunk):
    energy, col_sum, held, arrived = refs[-4:]
    copies = fetch(protos, held, arrived, chunk)
    teacher, _ = unit_rows(feats[...])
    for at in range(0, held.shape[1], size):
        if at % chunk == 0:
            copies[at // chunk].wait()
        unit, _ = unit_columns(held[:, at : at + size])
        score = jnp.dot(teacher, unit, preferred_element_type=F32)
        value = jnp.exp2(score * (TEACHER_SCALE * LOG2E))
        energy[:, at : at + size] = value.astype(BF16)
        col_sum[:, at : at + size] = jnp.sum(value, axis=0, keepdims=True)


def energy_call(place, feats, protos, after=(), size=512, chunk=2048):
    rows, width = feats.shape
    count = protos.shape[1]
    return pl.pallas_call(
        functools.partial(energy_kernel, size=size, chunk=chunk),
        in_specs=[SCALARS, WHOLE, ANY] + [ANY] * len(after),
        out_specs=[WHOLE, WHOLE],
        out_shape=[pltpu.VMEM((rows, count), BF16), jax.ShapeDtypeStruct((1, count), F32)],
        scratch_shapes=[pltpu.VMEM((width, count), BF16), pltpu.SemaphoreType.DMA((count // chunk,))],
        compiler_params=params(10),
        cost_estimate=cost(5.0),
        name="energy",
    )(place, in_hbm(feats), in_hbm(protos), *after)


def units_kernel(place, teacher, student, *refs):
    mine, other = refs[-2:]
    rows, width = mine.shape
    for side, target in ((place[1], mine), (1 - place[1], other)):
        here = pl.ds(pl.multiple_of(side * rows, rows), rows)
        target[:, : width // 2] = unit_rows(teacher[here, :])[0].astype(F32)
        target[:, width // 2 :] = unit_rows(student[here, :])[0].astype(F32)


def units_call(place, teacher, student, after=()):
    rows, width = teacher.shape
    return pl.pallas_call(
        units_kernel,
        in_specs=[SCALARS, WHOLE, WHOLE] + [ANY] * len(after),
        out_specs=[WHOLE] * 2,
        out_shape=[jax.ShapeDtypeStruct((rows // 2, 2 * width), F32)] * 2,
        compiler_params=params(8),
        cost_estimate=cost(1.5),
        name="units",
    )(place, in_hbm(teacher), in_hbm(student), *after)


def add_kernel(first, second, third, fourth, *refs):
    refs[-1][...] = (first[...] + second[...]) + (third[...] + fourth[...])


def add_call(parts, after):
    return pl.pallas_call(
        add_kernel,
        in_specs=[WHOLE] * 4 + [ANY] * len(after),
        out_specs=WHOLE,
        out_shape=jax.ShapeDtypeStruct(parts[0].shape, F32),
        compiler_params=params(4),
        cost_estimate=cost(0.5),
        name="add",
    )(*parts, *after)


def student_kernel(feats, protos, *refs, size, chunk, start):
    feat_part, unit_out, row_sum, held, arrived = refs[-5:]
    copies = fetch(protos, held, arrived, chunk, start)
    student, _ = unit_rows(feats[...])
    total = jnp.zeros((feats.shape[0], 128), F32)
    for at in range(0, held.shape[1], size):
        if at % chunk == 0:
            copies[at // chunk].wait()
        unit, _ = unit_columns(held[:, at : at + size])
        unit_out[:, at : at + size] = unit
        score = jnp.dot(student, unit, preferred_element_type=F32)
        value = jnp.exp2(score * (STUDENT_SCALE * LOG2E))
        part = lax.dot_general(value.astype(BF16), unit, (((1,), (1,)), ((), ())), preferred_element_type=F32)
        feat_part[...] = feat_part[...] + part if at else part
        for tile in range(0, size, 128):
            total = total + value[:, tile : tile + 128]
    row_sum[...] = jnp.sum(total.T, axis=0, keepdims=True)


def student_call(feats, protos, part, parts, after=(), size=512, chunk=1024):
    rows, width = feats.shape
    count = protos.shape[1] // parts
    return pl.pallas_call(
        functools.partial(student_kernel, size=size, chunk=chunk, start=part * count),
        in_specs=[WHOLE, ANY] + [ANY] * len(after),
        out_specs=[WHOLE] * 3,
        out_shape=[
            jax.ShapeDtypeStruct((rows, width), F32),
            pltpu.VMEM((width, count), BF16),
            jax.ShapeDtypeStruct((1, rows), F32),
        ],
        scratch_shapes=[pltpu.VMEM((width, count), BF16), pltpu.SemaphoreType.DMA((count // chunk,))],
        compiler_params=params(10),
        cost_estimate=cost(2.0),
        name="student",
    )(in_hbm(feats), in_hbm(protos), *after)


def tall_kernel(place, protos, *refs, pieces, turn, scale, size=512):
    energy = refs[len(refs) - 3 - turn]
    held, arrived = refs[-2:]
    rows = refs[0].shape[0]
    width, count = held.shape
    (copy,) = fetch(protos, held, arrived, count, pl.multiple_of(place[0] * count, count))
    side = slice(width, 2 * width) if turn else slice(0, width)
    feats = [refs[k][:, side] for k in range(pieces)]
    if turn:
        turned = refs[-3]
        for k in range(pieces):
            turned[:, k * rows : (k + 1) * rows] = feats[k].T.astype(BF16)
    feats = [value.astype(BF16) for value in feats]
    copy.wait()
    for at in range(0, count, size):
        unit, _ = unit_columns(held[:, at : at + size])
        for k in range(pieces):
            score = jnp.dot(feats[k], unit, preferred_element_type=F32)
            energy[k * rows : (k + 1) * rows, at : at + size] = jnp.exp2(score * (scale * LOG2E)).astype(BF16)


def tall_call(place, protos, feats, turn, scale, name, after=()):
    rows = feats[0].shape[0] * len(feats)
    width, count = protos.shape
    count = count // 4
    out_shape = [pltpu.VMEM((rows, count), BF16)]
    if turn:
        out_shape.append(jax.ShapeDtypeStruct((width, rows), BF16))
    return pl.pallas_call(
        functools.partial(tall_kernel, pieces=len(feats), turn=turn, scale=scale),
        in_specs=[SCALARS, ANY] + [WHOLE] * len(feats) + [ANY] * len(after),
        out_specs=[WHOLE] * len(out_shape),
        out_shape=out_shape,
        scratch_shapes=[pltpu.VMEM((width, count), BF16), pltpu.SemaphoreType.DMA((1,))],
        compiler_params=params(10),
        cost_estimate=cost(2.5),
        name=name,
    )(place, in_hbm(protos), *feats, *after)


def row_kernel(energy, col_total, *refs, total_protos, size=1024):
    row_part = refs[-1]
    rows, count = energy.shape
    total = jnp.zeros((16, rows), F32)
    for at in range(0, count, size):
        scale = two_terms(1.0 / (total_protos * col_total[:, at : at + size]))
        total = total + lax.dot_general(
            scale, energy[:, at : at + size], (((1,), (1,)), ((), ())), preferred_element_type=F32
        )
    row_part[...] = jnp.sum(total, axis=0, keepdims=True)


def row_call(energy, col_total, total_protos, after=()):
    return pl.pallas_call(
        functools.partial(row_kernel, total_protos=total_protos),
        in_specs=[WHOLE, WHOLE] + [ANY] * len(after),
        out_specs=WHOLE,
        out_shape=jax.ShapeDtypeStruct((1, energy.shape[0]), F32),
        compiler_params=params(4),
        name="row_pass",
    )(in_vmem(energy), col_total, *after)


def col_kernel(energy, row_total, *refs, total_rows, size=1024):
    col_part = refs[-1]
    scale = two_terms(1.0 / (total_rows * row_total[...]))
    for at in range(0, energy.shape[1], size):
        part = jnp.dot(scale, energy[:, at : at + size], preferred_element_type=F32)
        col_part[:, at : at + size] = jnp.sum(part, axis=0, keepdims=True)


def col_call(energy, row_total, total_rows, after=()):
    return pl.pallas_call(
        functools.partial(col_kernel, total_rows=total_rows),
        in_specs=[WHOLE, WHOLE] + [ANY] * len(after),
        out_specs=WHOLE,
        out_shape=jax.ShapeDtypeStruct((1, energy.shape[1]), F32),
        compiler_params=params(4),
        name="col_pass",
    )(in_vmem(energy), row_total, *after)


def target_kernel(energy, col_total, *refs, parts, total_protos, size):
    unit = refs[:parts]
    feat_part = refs[-1]
    count = unit[0].shape[1]
    for at in range(0, energy.shape[1], size):
        here = slice(at % count, at % count + size)
        scale = 1.0 / (total_protos * col_total[:, at : at + size])
        scaled = (unit[at // count][:, here].astype(F32) * scale).astype(BF16)
        part = lax.dot_general(energy[:, at : at + size], scaled, (((1,), (1,)), ((), ())), preferred_element_type=F32)
        feat_part[...] = feat_part[...] + part if at else part


def target_call(energy, unit, col_total, total_protos, after=(), size=1024):
    parts = len(unit)
    return pl.pallas_call(
        functools.partial(target_kernel, parts=parts, total_protos=total_protos, size=size),
        in_specs=[WHOLE] * (2 + parts) + [ANY] * len(after),
        out_specs=WHOLE,
        out_shape=jax.ShapeDtypeStruct((energy.shape[0], unit[0].shape[0]), F32),
        compiler_params=params(10),
        cost_estimate=cost(3.0),
        name="feat_target",
    )(in_vmem(energy), col_total, *[in_vmem(part) for part in unit], *after)


def mix_kernel(place, target, totals, *refs, parts):
    prob = refs[:parts]
    mine, other, total = refs[-3:]
    wide = target.shape[1] // 128
    rows_r = jnp.concatenate([across(STUDENT_SCALE / totals[:1, :])] * wide, axis=1)
    rows_s = jnp.concatenate([across(STUDENT_SCALE / totals[1:, :])] * wide, axis=1)
    whole = prob[0][...]
    for part in prob[1:]:
        whole = whole + part[...]
    total[...] = whole * rows_s - target[...] * rows_r
    rows = mine.shape[0]
    mine[...] = total[pl.ds(pl.multiple_of(place[1] * rows, rows), rows), :]
    other[...] = total[pl.ds(pl.multiple_of((1 - place[1]) * rows, rows), rows), :]


def mix_call(place, target, totals, prob):
    rows, width = target.shape
    return pl.pallas_call(
        functools.partial(mix_kernel, parts=len(prob)),
        in_specs=[SCALARS] + [WHOLE] * (2 + len(prob)),
        out_specs=[WHOLE] * 2,
        out_shape=[jax.ShapeDtypeStruct((rows // 2, width), F32)] * 2,
        scratch_shapes=[pltpu.VMEM((rows, width), F32)],
        compiler_params=params(10),
        cost_estimate=cost(1.0),
        name="feat_mix",
    )(place, target, totals, *prob)


def proto_kernel(place, protos, col_total, *refs, pieces, total_protos, size):
    energy, expo, turned, totals = refs[:2], refs[2:4], refs[4:6], refs[6 : 6 + pieces]
    grad, held, made, row_scale, soft_scale, arrived, left = refs[-7:]
    width, count = held.shape
    first = pl.multiple_of(place[0] * count, count)
    (copy,) = fetch(protos, held, arrived, count, first)
    tall = energy[0].shape[0]
    rows = tall // pieces
    for k in range(pieces):
        for half in range(2):
            side = jnp.where(place[1] == half, 0, 1)
            turn = (pieces - k) % pieces if half else k
            there = pl.ds(pl.multiple_of(side * tall + turn * rows, rows), rows)
            own = STUDENT_SCALE / totals[k][:, half * rows : (half + 1) * rows]
            row_scale[:, there] = own[:1]
            soft_scale[:, there] = own[1:]
    scaled = []
    for side in range(2):
        there = slice(side * tall, (side + 1) * tall)
        wide = turned[side][...].astype(F32)
        scaled.append(((wide * row_scale[:, there]).astype(BF16), (wide * soft_scale[:, there]).astype(BF16)))
    copies = []
    for at in range(0, count, size):
        here = slice(at, at + size)
        scale = 1.0 / (total_protos * col_total[:, pl.ds(first + at, size)])
        target = jnp.dot(scaled[0][0], energy[0][:, here], preferred_element_type=F32)
        target = target + jnp.dot(scaled[1][0], energy[1][:, here], preferred_element_type=F32)
        part = jnp.dot(scaled[0][1], expo[0][:, here], preferred_element_type=F32)
        part = part + jnp.dot(scaled[1][1], expo[1][:, here], preferred_element_type=F32)
        part = part - target * scale
        if at == 0:
            copy.wait()
        unit, norm = unit_columns(held[:, here])
        wide_unit = unit.astype(F32)
        dots = jnp.sum(wide_unit * part, axis=0, keepdims=True)
        made[:, here] = (part - wide_unit * dots) * (1.0 / norm)
        copies.append(pltpu.make_async_copy(made.at[:, here], grad.at[:, here], left.at[at // size]))
        copies[-1].start()
    for copy in copies:
        copy.wait()


def proto_call(place, protos, energy, expo, turned, col_total, totals, total_protos, after=(), size=512):
    rows, count = energy[0].shape
    width = protos.shape[0]
    return pl.pallas_call(
        functools.partial(proto_kernel, pieces=len(totals), total_protos=total_protos, size=size),
        in_specs=[SCALARS, ANY] + [WHOLE] * (7 + len(totals)) + [ANY] * len(after),
        out_specs=ANY,
        out_shape=pltpu.HBM((width, count), F32),
        scratch_shapes=[
            pltpu.VMEM((width, count), BF16),
            pltpu.VMEM((width, count), F32),
            pltpu.VMEM((1, 2 * rows), F32),
            pltpu.VMEM((1, 2 * rows), F32),
            pltpu.SemaphoreType.DMA((1,)),
            pltpu.SemaphoreType.DMA((count // size,)),
        ],
        compiler_params=params(20),
        cost_estimate=cost(8.0),
        name="proto_grad",
    )(
        place, in_hbm(protos), col_total, *[in_vmem(part) for part in energy], *[in_vmem(part) for part in expo],
        *turned, *totals, *after,
    )


def finish_kernel(place, feats, first, second, third, fourth, grad):
    rows = grad.shape[0]
    here = pl.ds(pl.multiple_of(place[1] * rows, rows), rows)
    unit, norm = unit_rows(feats[here, :])
    unit = unit.astype(F32)
    feat_sum = (first[...] + second[...]) + (third[...] + fourth[...])
    along = jnp.sum(unit * feat_sum, axis=1, keepdims=True)
    grad[...] = (feat_sum - unit * along) / norm


def finish_call(place, feats, parts):
    return pl.pallas_call(
        finish_kernel,
        in_specs=[SCALARS] + [WHOLE] * (1 + len(parts)),
        out_specs=WHOLE,
        out_shape=jax.ShapeDtypeStruct(parts[0].shape, F32),
        compiler_params=params(8),
        cost_estimate=cost(1.0),
        name="finish",
    )(place, feats, *parts)


def join_kernel(place, mine, other, whole):
    rows = mine.shape[0]
    whole[pl.ds(pl.multiple_of(place[1] * rows, rows), rows), :] = mine[...]
    whole[pl.ds(pl.multiple_of((1 - place[1]) * rows, rows), rows), :] = other[...]


def join_call(place, mine, other):
    rows, width = mine.shape
    return pl.pallas_call(
        join_kernel,
        in_specs=[SCALARS, WHOLE, WHOLE],
        out_specs=WHOLE,
        out_shape=jax.ShapeDtypeStruct((2 * rows, width), F32),
        compiler_params=params(8),
        cost_estimate=cost(1.0),
        name="join",
    )(place, mine, other)


def shifted(value, axis, shift):
    size = SIZES[axis]
    return lax.ppermute(value, axis, [(i, (i + shift) % size) for i in range(size)])


def two_way(value):
    pairs = []
    for z in range(4):
        pairs.append((2 * z, 2 * ((z + 1) % 4)))
        pairs.append((2 * z + 1, 2 * ((z + 3) % 4) + 1))
    return lax.ppermute(value, ("z", "core"), pairs)


def ring_parts(value, axis):
    made = {shift: shifted(value, axis, shift) for shift in ((1, 3, 2) if SIZES[axis] == 4 else (1,))}
    return [value] + [made[shift] for shift in sorted(made)]


def ring_sum(value, axis):
    parts = ring_parts(value, axis)
    value = parts[0]
    for part in parts[1:]:
        value = value + part
    return value


def batch_sum(value):
    return ring_sum(ring_sum(value, "x"), "z")


def x_sum(value, after):
    return add_call(ring_parts(value, "x"), after)


def proto_sum(value):
    return ring_sum(ring_sum(value, "core"), "y")


def on_device(student_feats, teacher_feats, protos, teacher_protos):
    rows, width = student_feats.shape
    count = protos.shape[1]
    total_rows = rows * 16
    total_protos = count * 8
    place = jnp.stack([lax.axis_index("z"), lax.axis_index("core")]).astype(jnp.int32)

    near, far = units_call(place, teacher_feats, student_feats)
    first = two_way(near)
    energy, col_part = energy_call(place, teacher_feats, teacher_protos)
    col_total = batch_sum(col_part)
    second = two_way(first)
    feat_prob, unit, soft_part = student_call(student_feats, protos, 0, 1, (col_part,))
    row_part = row_call(energy, col_total, total_protos, (soft_part, first))
    row_total = proto_sum(row_part)
    third = two_way(second)
    col_part = col_call(energy, row_total, total_rows, (second,))
    col_total = batch_sum(col_part)
    row_part = row_call(energy, col_total, total_protos, (third,))
    near_side = [near, first, second, third]
    far_side = [far] + [shifted(part, "core", 1) for part in (first, second, third)]
    row_total = proto_sum(row_part)
    near_expo, near_turned = tall_call(place, protos, near_side, 1, STUDENT_SCALE, "tall_expo", (row_part,))
    col_part = col_call(energy, row_total, total_rows, (near_turned,))
    far_expo, far_turned = tall_call(place, protos, far_side, 1, STUDENT_SCALE, "tall_expo", (col_part,))
    col_half = x_sum(col_part, (far_turned,))
    (near_energy,) = tall_call(place, teacher_protos, near_side, 0, TEACHER_SCALE, "tall_energy", (col_half,))
    col_total = ring_sum(col_half, "z")
    row_part = row_call(energy, col_total, total_protos, (near_energy,))
    feat_target = target_call(energy, [unit], col_total, total_protos, (row_part,))
    totals = proto_sum(jnp.concatenate([row_part, soft_part], axis=0))
    mine, other = mix_call(place, feat_target, totals, [feat_prob])
    feat_half = mine + shifted(other, "core", 1)
    (far_energy,) = tall_call(place, teacher_protos, far_side, 0, TEACHER_SCALE, "tall_energy", (totals,))
    grad_part = proto_call(
        place, protos, [near_energy, far_energy], [near_expo, far_expo], [near_turned, far_turned], col_total,
        ring_parts(totals, "z"), total_protos, (feat_half,),
    )
    pieces = lax.all_to_all(grad_part.reshape(16, width // 16, count // 4), BATCH, 0, 0)
    pieces = jnp.sum(pieces.reshape(4, 4, width // 16, count // 4), axis=0)
    grad_protos = pieces.transpose(1, 0, 2).reshape(width // 16, count)

    grad_half = finish_call(place, student_feats, ring_parts(feat_half, "y"))
    return join_call(place, grad_half, shifted(grad_half, "core", 1)), grad_protos


def solution(mesh):
    split = Mesh(mesh.devices.reshape(4, 4, 4, 2), ("x", "z", "y", "core"))
    return jax.shard_map(
        on_device,
        mesh=split,
        in_specs=(P(BATCH, None), P(BATCH, None), P(None, PROTO), P(None, PROTO)),
        out_specs=(P(BATCH, None), P(BATCH, PROTO)),
        check_vma=False,
    )
```

```python
import functools

import jax
import jax.numpy as jnp
from jax import lax
from jax.experimental import pallas as pl
from jax.experimental.pallas import tpu as pltpu
from jax.sharding import Mesh
from jax.sharding import PartitionSpec as P

EPSILON = 1e-06
TEACHER_SCALE = 25.0
STUDENT_SCALE = 10.0
LOG2E = 1.4426950408889634
SIZES = {"x": 4, "z": 4, "y": 4, "core": 2}
BATCH = ("x", "z")
PROTO = ("y", "core")
WHOLE = pl.BlockSpec(memory_space=pltpu.VMEM)
SCALARS = pl.BlockSpec(memory_space=pltpu.SMEM)
ANY = pl.BlockSpec(memory_space=pl.ANY)
F32 = jnp.float32
BF16 = jnp.bfloat16


def params(mib):
    return pltpu.CompilerParams(vmem_limit_bytes=mib << 20)


def cost(microseconds):
    return pl.CostEstimate(flops=0, bytes_accessed=int(microseconds * 3.0e6), transcendentals=0)


def in_vmem(value):
    return pltpu.with_memory_space_constraint(value, pltpu.VMEM)


def in_hbm(value):
    return pltpu.with_memory_space_constraint(value, pltpu.HBM)


def unit_rows(values):
    wide = values.astype(F32)
    norms = jnp.sqrt(jnp.sum(wide * wide, axis=1, keepdims=True) + EPSILON)
    return (wide / norms).astype(BF16), norms


def unit_columns(values):
    wide = values.astype(F32)
    norms = jnp.sqrt(jnp.sum(wide * wide, axis=0, keepdims=True) + EPSILON)
    return (wide * (1.0 / norms)).astype(BF16), norms


def across(row, lanes=128):
    return jnp.broadcast_to(row, (lanes, row.shape[1])).T


def two_terms(row):
    high = row.astype(BF16).astype(F32)
    place = lax.broadcasted_iota(jnp.int32, (16, row.shape[1]), 0)
    return jnp.where(place == 0, high, jnp.where(place == 1, row - high, 0.0)).astype(BF16)


def fetch(source, held, arrived, chunk, start=0):
    copies = [
        pltpu.make_async_copy(
            source.at[:, pl.ds(start + at, chunk)], held.at[:, at : at + chunk], arrived.at[at // chunk]
        )
        for at in range(0, held.shape[1], chunk)
    ]
    for copy in copies:
        copy.start()
    return copies


def energy_kernel(place, feats, protos, *refs, size, chunk):
    energy, col_sum, held, arrived = refs[-4:]
    copies = fetch(protos, held, arrived, chunk)
    teacher, _ = unit_rows(feats[...])
    for at in range(0, held.shape[1], size):
        if at % chunk == 0:
            copies[at // chunk].wait()
        unit, _ = unit_columns(held[:, at : at + size])
        score = jnp.dot(teacher, unit, preferred_element_type=F32)
        value = jnp.exp2(score * (TEACHER_SCALE * LOG2E))
        energy[:, at : at + size] = value.astype(BF16)
        col_sum[:, at : at + size] = jnp.sum(value, axis=0, keepdims=True)


def energy_call(place, feats, protos, after=(), size=512, chunk=2048):
    rows, width = feats.shape
    count = protos.shape[1]
    return pl.pallas_call(
        functools.partial(energy_kernel, size=size, chunk=chunk),
        in_specs=[SCALARS, WHOLE, ANY] + [ANY] * len(after),
        out_specs=[WHOLE, WHOLE],
        out_shape=[pltpu.VMEM((rows, count), BF16), jax.ShapeDtypeStruct((1, count), F32)],
        scratch_shapes=[pltpu.VMEM((width, count), BF16), pltpu.SemaphoreType.DMA((count // chunk,))],
        compiler_params=params(10),
        cost_estimate=cost(5.0),
        name="energy",
    )(place, in_hbm(feats), in_hbm(protos), *after)


def units_kernel(place, teacher, student, *refs):
    mine, other = refs[-2:]
    rows, width = mine.shape
    for side, target in ((place[1], mine), (1 - place[1], other)):
        here = pl.ds(pl.multiple_of(side * rows, rows), rows)
        target[:, : width // 2] = unit_rows(teacher[here, :])[0].astype(F32)
        target[:, width // 2 :] = unit_rows(student[here, :])[0].astype(F32)


def units_call(place, teacher, student, after=()):
    rows, width = teacher.shape
    return pl.pallas_call(
        units_kernel,
        in_specs=[SCALARS, WHOLE, WHOLE] + [ANY] * len(after),
        out_specs=[WHOLE] * 2,
        out_shape=[jax.ShapeDtypeStruct((rows // 2, 2 * width), F32)] * 2,
        compiler_params=params(8),
        cost_estimate=cost(1.5),
        name="units",
    )(place, teacher, student, *after)


def add_kernel(first, second, third, fourth, *refs):
    refs[-1][...] = (first[...] + second[...]) + (third[...] + fourth[...])


def add_call(parts, after):
    return pl.pallas_call(
        add_kernel,
        in_specs=[WHOLE] * 4 + [ANY] * len(after),
        out_specs=WHOLE,
        out_shape=jax.ShapeDtypeStruct(parts[0].shape, F32),
        compiler_params=params(4),
        cost_estimate=cost(0.5),
        name="add",
    )(*parts, *after)


def student_kernel(feats, protos, *refs, size, chunk, start):
    feat_part, unit_out, row_sum, held, arrived = refs[-5:]
    copies = fetch(protos, held, arrived, chunk, start)
    student, _ = unit_rows(feats[...])
    total = jnp.zeros((feats.shape[0], 128), F32)
    for at in range(0, held.shape[1], size):
        if at % chunk == 0:
            copies[at // chunk].wait()
        unit, _ = unit_columns(held[:, at : at + size])
        unit_out[:, at : at + size] = unit
        score = jnp.dot(student, unit, preferred_element_type=F32)
        value = jnp.exp2(score * (STUDENT_SCALE * LOG2E))
        part = lax.dot_general(value.astype(BF16), unit, (((1,), (1,)), ((), ())), preferred_element_type=F32)
        feat_part[...] = feat_part[...] + part if at else part
        for tile in range(0, size, 128):
            total = total + value[:, tile : tile + 128]
    row_sum[...] = jnp.sum(total.T, axis=0, keepdims=True)


def student_call(feats, protos, part, parts, after=(), size=512, chunk=1024):
    rows, width = feats.shape
    count = protos.shape[1] // parts
    return pl.pallas_call(
        functools.partial(student_kernel, size=size, chunk=chunk, start=part * count),
        in_specs=[WHOLE, ANY] + [ANY] * len(after),
        out_specs=[WHOLE] * 3,
        out_shape=[
            jax.ShapeDtypeStruct((rows, width), F32),
            pltpu.VMEM((width, count), BF16),
            jax.ShapeDtypeStruct((1, rows), F32),
        ],
        scratch_shapes=[pltpu.VMEM((width, count), BF16), pltpu.SemaphoreType.DMA((count // chunk,))],
        compiler_params=params(10),
        cost_estimate=cost(2.0),
        name="student",
    )(feats, in_hbm(protos), *after)


def tall_kernel(place, protos, *refs, pieces, turn, scale, size=512):
    energy = refs[len(refs) - 3 - turn]
    held, arrived = refs[-2:]
    rows = refs[0].shape[0]
    width, count = held.shape
    (copy,) = fetch(protos, held, arrived, count, pl.multiple_of(place[0] * count, count))
    side = slice(width, 2 * width) if turn else slice(0, width)
    feats = [refs[k][:, side] for k in range(pieces)]
    if turn:
        turned = refs[-3]
        for k in range(pieces):
            turned[:, k * rows : (k + 1) * rows] = feats[k].T.astype(BF16)
    feats = [value.astype(BF16) for value in feats]
    copy.wait()
    for at in range(0, count, size):
        unit, _ = unit_columns(held[:, at : at + size])
        for k in range(pieces):
            score = jnp.dot(feats[k], unit, preferred_element_type=F32)
            energy[k * rows : (k + 1) * rows, at : at + size] = jnp.exp2(score * (scale * LOG2E)).astype(BF16)


def tall_call(place, protos, feats, turn, scale, name, after=()):
    rows = feats[0].shape[0] * len(feats)
    width, count = protos.shape
    count = count // 4
    out_shape = [pltpu.VMEM((rows, count), BF16)]
    if turn:
        out_shape.append(jax.ShapeDtypeStruct((width, rows), BF16))
    return pl.pallas_call(
        functools.partial(tall_kernel, pieces=len(feats), turn=turn, scale=scale),
        in_specs=[SCALARS, ANY] + [WHOLE] * len(feats) + [ANY] * len(after),
        out_specs=[WHOLE] * len(out_shape),
        out_shape=out_shape,
        scratch_shapes=[pltpu.VMEM((width, count), BF16), pltpu.SemaphoreType.DMA((1,))],
        compiler_params=params(10),
        cost_estimate=cost(2.5),
        name=name,
    )(place, in_hbm(protos), *feats, *after)


def row_kernel(energy, col_total, *refs, total_protos, size=512):
    row_part, lanes, scales = refs[-3:]
    rows, count = energy.shape
    cut = count // 2
    scales[...] = jnp.broadcast_to(1.0 / (total_protos * col_total[:, cut:]), scales.shape)
    total = jnp.zeros((16, rows), F32)
    steps = cut // size
    groups = rows // 16 // steps
    for step in range(steps):
        at = step * size
        scale = two_terms(1.0 / (total_protos * col_total[:, at : at + size]))
        total = total + lax.dot_general(
            scale, energy[:, at : at + size], (((1,), (1,)), ((), ())), preferred_element_type=F32
        )
        for group in range(step * groups, (step + 1) * groups):
            here = slice(group * 16, (group + 1) * 16)
            sums = [jnp.zeros((16, 128), F32)] * 2
            for tile in range((count - cut) // 128):
                lane = slice(tile * 128, (tile + 1) * 128)
                value = energy[here, cut + tile * 128 : cut + (tile + 1) * 128].astype(F32)
                sums[tile % 2] = sums[tile % 2] + value * scales[:, lane]
            lanes[here, :] = sums[0] + sums[1]
    row_part[...] = jnp.sum(total, axis=0, keepdims=True) + jnp.sum(lanes[...].T, axis=0, keepdims=True)


def row_call(energy, col_total, total_protos, after=()):
    rows, count = energy.shape
    return pl.pallas_call(
        functools.partial(row_kernel, total_protos=total_protos),
        in_specs=[WHOLE, WHOLE] + [ANY] * len(after),
        out_specs=WHOLE,
        out_shape=jax.ShapeDtypeStruct((1, rows), F32),
        scratch_shapes=[pltpu.VMEM((rows, 128), F32), pltpu.VMEM((16, count // 2), F32)],
        compiler_params=params(6),
        name="row_pass",
    )(in_vmem(energy), col_total, *after)


def col_kernel(energy, row_total, *refs, total_rows, size=1024):
    col_part = refs[-1]
    scale = two_terms(1.0 / (total_rows * row_total[...]))
    for at in range(0, energy.shape[1], size):
        part = jnp.dot(scale, energy[:, at : at + size], preferred_element_type=F32)
        col_part[:, at : at + size] = jnp.sum(part, axis=0, keepdims=True)


def col_call(energy, row_total, total_rows, after=()):
    return pl.pallas_call(
        functools.partial(col_kernel, total_rows=total_rows),
        in_specs=[WHOLE, WHOLE] + [ANY] * len(after),
        out_specs=WHOLE,
        out_shape=jax.ShapeDtypeStruct((1, energy.shape[1]), F32),
        compiler_params=params(4),
        name="col_pass",
    )(in_vmem(energy), row_total, *after)


def target_kernel(energy, col_total, *refs, parts, total_protos, size):
    unit = refs[:parts]
    feat_part = refs[-1]
    count = unit[0].shape[1]
    for at in range(0, energy.shape[1], size):
        here = slice(at % count, at % count + size)
        scale = 1.0 / (total_protos * col_total[:, at : at + size])
        scaled = (unit[at // count][:, here].astype(F32) * scale).astype(BF16)
        part = lax.dot_general(energy[:, at : at + size], scaled, (((1,), (1,)), ((), ())), preferred_element_type=F32)
        feat_part[...] = feat_part[...] + part if at else part


def target_call(energy, unit, col_total, total_protos, after=(), size=1024):
    parts = len(unit)
    return pl.pallas_call(
        functools.partial(target_kernel, parts=parts, total_protos=total_protos, size=size),
        in_specs=[WHOLE] * (2 + parts) + [ANY] * len(after),
        out_specs=WHOLE,
        out_shape=jax.ShapeDtypeStruct((energy.shape[0], unit[0].shape[0]), F32),
        compiler_params=params(10),
        cost_estimate=cost(3.0),
        name="feat_target",
    )(in_vmem(energy), col_total, *[in_vmem(part) for part in unit], *after)


def mix_kernel(place, target, totals, *refs, parts):
    prob = refs[:parts]
    mine, other, total = refs[-3:]
    wide = target.shape[1] // 128
    rows_r = jnp.concatenate([across(STUDENT_SCALE / totals[:1, :])] * wide, axis=1)
    rows_s = jnp.concatenate([across(STUDENT_SCALE / totals[1:, :])] * wide, axis=1)
    whole = prob[0][...]
    for part in prob[1:]:
        whole = whole + part[...]
    total[...] = whole * rows_s - target[...] * rows_r
    rows = mine.shape[0]
    mine[...] = total[pl.ds(pl.multiple_of(place[1] * rows, rows), rows), :]
    other[...] = total[pl.ds(pl.multiple_of((1 - place[1]) * rows, rows), rows), :]


def mix_call(place, target, totals, prob):
    rows, width = target.shape
    return pl.pallas_call(
        functools.partial(mix_kernel, parts=len(prob)),
        in_specs=[SCALARS] + [WHOLE] * (2 + len(prob)),
        out_specs=[WHOLE] * 2,
        out_shape=[jax.ShapeDtypeStruct((rows // 2, width), F32)] * 2,
        scratch_shapes=[pltpu.VMEM((rows, width), F32)],
        compiler_params=params(10),
        cost_estimate=cost(1.0),
        name="feat_mix",
    )(place, target, totals, *prob)


def proto_kernel(place, protos, col_total, *refs, pieces, total_protos, size):
    energy, expo, turned, totals = refs[:2], refs[2:4], refs[4:6], refs[6 : 6 + pieces]
    grad, held, made, row_scale, soft_scale, arrived, left = refs[-7:]
    width, count = held.shape
    first = pl.multiple_of(place[0] * count, count)
    (copy,) = fetch(protos, held, arrived, count, first)
    tall = energy[0].shape[0]
    rows = tall // pieces
    for k in range(pieces):
        for half in range(2):
            side = jnp.where(place[1] == half, 0, 1)
            turn = (pieces - k) % pieces if half else k
            there = pl.ds(pl.multiple_of(side * tall + turn * rows, rows), rows)
            own = STUDENT_SCALE / totals[k][:, half * rows : (half + 1) * rows]
            row_scale[:, there] = own[:1]
            soft_scale[:, there] = own[1:]
    scaled = []
    for side in range(2):
        there = slice(side * tall, (side + 1) * tall)
        wide = turned[side][...].astype(F32)
        scaled.append(((wide * row_scale[:, there]).astype(BF16), (wide * soft_scale[:, there]).astype(BF16)))
    copies = []
    for at in range(0, count, size):
        here = slice(at, at + size)
        scale = 1.0 / (total_protos * col_total[:, pl.ds(first + at, size)])
        target = jnp.dot(scaled[0][0], energy[0][:, here], preferred_element_type=F32)
        target = target + jnp.dot(scaled[1][0], energy[1][:, here], preferred_element_type=F32)
        part = jnp.dot(scaled[0][1], expo[0][:, here], preferred_element_type=F32)
        part = part + jnp.dot(scaled[1][1], expo[1][:, here], preferred_element_type=F32)
        part = part - target * scale
        if at == 0:
            copy.wait()
        unit, norm = unit_columns(held[:, here])
        wide_unit = unit.astype(F32)
        dots = jnp.sum(wide_unit * part, axis=0, keepdims=True)
        made[:, here] = (part - wide_unit * dots) * (1.0 / norm)
        copies.append(pltpu.make_async_copy(made.at[:, here], grad.at[:, here], left.at[at // size]))
        copies[-1].start()
    for copy in copies:
        copy.wait()


def proto_call(place, protos, energy, expo, turned, col_total, totals, total_protos, after=(), size=512):
    rows, count = energy[0].shape
    width = protos.shape[0]
    return pl.pallas_call(
        functools.partial(proto_kernel, pieces=len(totals), total_protos=total_protos, size=size),
        in_specs=[SCALARS, ANY] + [WHOLE] * (7 + len(totals)) + [ANY] * len(after),
        out_specs=ANY,
        out_shape=pltpu.HBM((width, count), F32),
        scratch_shapes=[
            pltpu.VMEM((width, count), BF16),
            pltpu.VMEM((width, count), F32),
            pltpu.VMEM((1, 2 * rows), F32),
            pltpu.VMEM((1, 2 * rows), F32),
            pltpu.SemaphoreType.DMA((1,)),
            pltpu.SemaphoreType.DMA((count // size,)),
        ],
        compiler_params=params(20),
        cost_estimate=cost(8.0),
        name="proto_grad",
    )(
        place, in_hbm(protos), col_total, *[in_vmem(part) for part in energy], *[in_vmem(part) for part in expo],
        *turned, *totals, *after,
    )


def finish_kernel(place, feats, first, second, third, fourth, grad):
    rows = grad.shape[0]
    here = pl.ds(pl.multiple_of(place[1] * rows, rows), rows)
    unit, norm = unit_rows(feats[here, :])
    unit = unit.astype(F32)
    feat_sum = (first[...] + second[...]) + (third[...] + fourth[...])
    along = jnp.sum(unit * feat_sum, axis=1, keepdims=True)
    grad[...] = (feat_sum - unit * along) / norm


def finish_call(place, feats, parts):
    return pl.pallas_call(
        finish_kernel,
        in_specs=[SCALARS] + [WHOLE] * (1 + len(parts)),
        out_specs=WHOLE,
        out_shape=jax.ShapeDtypeStruct(parts[0].shape, F32),
        compiler_params=params(8),
        cost_estimate=cost(1.0),
        name="finish",
    )(place, feats, *parts)


def join_kernel(place, mine, other, whole):
    rows = mine.shape[0]
    whole[pl.ds(pl.multiple_of(place[1] * rows, rows), rows), :] = mine[...]
    whole[pl.ds(pl.multiple_of((1 - place[1]) * rows, rows), rows), :] = other[...]


def join_call(place, mine, other):
    rows, width = mine.shape
    return pl.pallas_call(
        join_kernel,
        in_specs=[SCALARS, WHOLE, WHOLE],
        out_specs=WHOLE,
        out_shape=jax.ShapeDtypeStruct((2 * rows, width), F32),
        compiler_params=params(8),
        cost_estimate=cost(1.0),
        name="join",
    )(place, mine, other)


def shifted(value, axis, shift):
    size = SIZES[axis]
    return lax.ppermute(value, axis, [(i, (i + shift) % size) for i in range(size)])


def two_way(value):
    pairs = []
    for z in range(4):
        pairs.append((2 * z, 2 * ((z + 1) % 4)))
        pairs.append((2 * z + 1, 2 * ((z + 3) % 4) + 1))
    return lax.ppermute(value, ("z", "core"), pairs)


def ring_parts(value, axis):
    made = {shift: shifted(value, axis, shift) for shift in ((1, 3, 2) if SIZES[axis] == 4 else (1,))}
    return [value] + [made[shift] for shift in sorted(made)]


def ring_sum(value, axis):
    parts = ring_parts(value, axis)
    value = parts[0]
    for part in parts[1:]:
        value = value + part
    return value


def batch_sum(value):
    return ring_sum(ring_sum(value, "x"), "z")


def x_sum(value, after):
    return add_call(ring_parts(value, "x"), after)


def proto_sum(value):
    return ring_sum(ring_sum(value, "core"), "y")


def on_device(student_feats, teacher_feats, protos, teacher_protos):
    rows, width = student_feats.shape
    count = protos.shape[1]
    total_rows = rows * 16
    total_protos = count * 8
    place = jnp.stack([lax.axis_index("z"), lax.axis_index("core")]).astype(jnp.int32)

    near, far = units_call(place, teacher_feats, student_feats)
    first = two_way(near)
    energy, col_part = energy_call(place, teacher_feats, teacher_protos)
    col_total = batch_sum(col_part)
    second = two_way(first)
    students = [student_call(student_feats, protos, 0, 2, (col_part,))]
    row_part = row_call(energy, col_total, total_protos, (students[0][2], first))
    students.append(student_call(student_feats, protos, 1, 2, (row_part,)))
    soft_part = students[0][2] + students[1][2]
    row_total = proto_sum(row_part)
    third = two_way(second)
    col_part = col_call(energy, row_total, total_rows, (second, students[1][2]))
    col_total = batch_sum(col_part)
    row_part = row_call(energy, col_total, total_protos, (third,))
    near_side = [near, first, second, third]
    far_side = [far] + [shifted(part, "core", 1) for part in (first, second, third)]
    row_total = proto_sum(row_part)
    near_expo, near_turned = tall_call(place, protos, near_side, 1, STUDENT_SCALE, "tall_expo", (row_part,))
    col_part = col_call(energy, row_total, total_rows, (near_turned,))
    far_expo, far_turned = tall_call(place, protos, far_side, 1, STUDENT_SCALE, "tall_expo", (col_part,))
    col_half = x_sum(col_part, (far_turned,))
    (near_energy,) = tall_call(place, teacher_protos, near_side, 0, TEACHER_SCALE, "tall_energy", (col_half,))
    col_total = ring_sum(col_half, "z")
    row_part = row_call(energy, col_total, total_protos, (near_energy,))
    feat_target = target_call(energy, [made[1] for made in students], col_total, total_protos, (row_part,))
    totals = proto_sum(jnp.concatenate([row_part, soft_part], axis=0))
    mine, other = mix_call(place, feat_target, totals, [made[0] for made in students])
    feat_half = mine + shifted(other, "core", 1)
    (far_energy,) = tall_call(place, teacher_protos, far_side, 0, TEACHER_SCALE, "tall_energy", (totals,))
    grad_part = proto_call(
        place, protos, [near_energy, far_energy], [near_expo, far_expo], [near_turned, far_turned], col_total,
        ring_parts(totals, "z"), total_protos, (feat_half,),
    )
    pieces = lax.all_to_all(grad_part.reshape(16, width // 16, count // 4), BATCH, 0, 0)
    pieces = jnp.sum(pieces.reshape(4, 4, width // 16, count // 4), axis=0)
    grad_protos = pieces.transpose(1, 0, 2).reshape(width // 16, count)

    grad_half = finish_call(place, student_feats, ring_parts(feat_half, "y"))
    return join_call(place, grad_half, shifted(grad_half, "core", 1)), grad_protos


def solution(mesh):
    split = Mesh(mesh.devices.reshape(4, 4, 4, 2), ("x", "z", "y", "core"))
    return jax.shard_map(
        on_device,
        mesh=split,
        in_specs=(P(BATCH, None), P(BATCH, None), P(None, PROTO), P(None, PROTO)),
        out_specs=(P(BATCH, None), P(BATCH, PROTO)),
        check_vma=False,
    )
```

```python
import functools

import jax
import jax.numpy as jnp
from jax import lax
from jax.experimental import pallas as pl
from jax.experimental.pallas import tpu as pltpu
from jax.sharding import Mesh
from jax.sharding import PartitionSpec as P

EPSILON = 1e-06
TEACHER_SCALE = 25.0
STUDENT_SCALE = 10.0
LOG2E = 1.4426950408889634
SIZES = {"x": 4, "z": 4, "y": 4, "core": 2}
BATCH = ("x", "z")
PROTO = ("y", "core")
WHOLE = pl.BlockSpec(memory_space=pltpu.VMEM)
SCALARS = pl.BlockSpec(memory_space=pltpu.SMEM)
ANY = pl.BlockSpec(memory_space=pl.ANY)
F32 = jnp.float32
BF16 = jnp.bfloat16


def params(mib):
    return pltpu.CompilerParams(vmem_limit_bytes=mib << 20)


def cost(microseconds):
    return pl.CostEstimate(flops=0, bytes_accessed=int(microseconds * 3.0e6), transcendentals=0)


def in_vmem(value):
    return pltpu.with_memory_space_constraint(value, pltpu.VMEM)


def in_hbm(value):
    return pltpu.with_memory_space_constraint(value, pltpu.HBM)


def unit_rows(values):
    wide = values.astype(F32)
    norms = jnp.sqrt(jnp.sum(wide * wide, axis=1, keepdims=True) + EPSILON)
    return (wide / norms).astype(BF16), norms


def unit_columns(values):
    wide = values.astype(F32)
    norms = jnp.sqrt(jnp.sum(wide * wide, axis=0, keepdims=True) + EPSILON)
    return (wide * (1.0 / norms)).astype(BF16), norms


def across(row, lanes=128):
    return jnp.broadcast_to(row, (lanes, row.shape[1])).T


def two_terms(row):
    high = row.astype(BF16).astype(F32)
    place = lax.broadcasted_iota(jnp.int32, (16, row.shape[1]), 0)
    return jnp.where(place == 0, high, jnp.where(place == 1, row - high, 0.0)).astype(BF16)


def fetch(source, held, arrived, chunk, start=0):
    copies = [
        pltpu.make_async_copy(
            source.at[:, pl.ds(start + at, chunk)], held.at[:, at : at + chunk], arrived.at[at // chunk]
        )
        for at in range(0, held.shape[1], chunk)
    ]
    for copy in copies:
        copy.start()
    return copies


def energy_kernel(place, feats, protos, *refs, size, chunk):
    energy, col_sum, held, arrived = refs[-4:]
    copies = fetch(protos, held, arrived, chunk)
    teacher, _ = unit_rows(feats[...])
    for at in range(0, held.shape[1], size):
        if at % chunk == 0:
            copies[at // chunk].wait()
        unit, _ = unit_columns(held[:, at : at + size])
        score = jnp.dot(teacher, unit, preferred_element_type=F32)
        value = jnp.exp2(score * (TEACHER_SCALE * LOG2E))
        energy[:, at : at + size] = value.astype(BF16)
        col_sum[:, at : at + size] = jnp.sum(value, axis=0, keepdims=True)


def energy_call(place, feats, protos, after=(), size=512, chunk=2048):
    rows, width = feats.shape
    count = protos.shape[1]
    return pl.pallas_call(
        functools.partial(energy_kernel, size=size, chunk=chunk),
        in_specs=[SCALARS, WHOLE, ANY] + [ANY] * len(after),
        out_specs=[WHOLE, WHOLE],
        out_shape=[pltpu.VMEM((rows, count), BF16), jax.ShapeDtypeStruct((1, count), F32)],
        scratch_shapes=[pltpu.VMEM((width, count), BF16), pltpu.SemaphoreType.DMA((count // chunk,))],
        compiler_params=params(10),
        cost_estimate=cost(5.0),
        name="energy",
    )(place, in_hbm(feats), in_hbm(protos), *after)


def units_kernel(place, teacher, student, *refs):
    mine, other = refs[-2:]
    rows, width = mine.shape
    for side, target in ((place[1], mine), (1 - place[1], other)):
        here = pl.ds(pl.multiple_of(side * rows, rows), rows)
        target[:, : width // 2] = unit_rows(teacher[here, :])[0].astype(F32)
        target[:, width // 2 :] = unit_rows(student[here, :])[0].astype(F32)


def units_call(place, teacher, student, after=()):
    rows, width = teacher.shape
    return pl.pallas_call(
        units_kernel,
        in_specs=[SCALARS, WHOLE, WHOLE] + [ANY] * len(after),
        out_specs=[WHOLE] * 2,
        out_shape=[jax.ShapeDtypeStruct((rows // 2, 2 * width), F32)] * 2,
        compiler_params=params(8),
        cost_estimate=cost(1.5),
        name="units",
    )(place, teacher, student, *after)


def add_kernel(first, second, third, fourth, *refs):
    refs[-1][...] = (first[...] + second[...]) + (third[...] + fourth[...])


def add_call(parts, after):
    return pl.pallas_call(
        add_kernel,
        in_specs=[WHOLE] * 4 + [ANY] * len(after),
        out_specs=WHOLE,
        out_shape=jax.ShapeDtypeStruct(parts[0].shape, F32),
        compiler_params=params(4),
        cost_estimate=cost(0.5),
        name="add",
    )(*parts, *after)


def student_kernel(feats, protos, *refs, size, chunk, start):
    feat_part, unit_out, row_sum, held, arrived = refs[-5:]
    copies = fetch(protos, held, arrived, chunk, start)
    student, _ = unit_rows(feats[...])
    total = jnp.zeros((feats.shape[0], 128), F32)
    for at in range(0, held.shape[1], size):
        if at % chunk == 0:
            copies[at // chunk].wait()
        unit, _ = unit_columns(held[:, at : at + size])
        unit_out[:, at : at + size] = unit
        score = jnp.dot(student, unit, preferred_element_type=F32)
        value = jnp.exp2(score * (STUDENT_SCALE * LOG2E))
        part = lax.dot_general(value.astype(BF16), unit, (((1,), (1,)), ((), ())), preferred_element_type=F32)
        feat_part[...] = feat_part[...] + part if at else part
        for tile in range(0, size, 128):
            total = total + value[:, tile : tile + 128]
    row_sum[...] = jnp.sum(total.T, axis=0, keepdims=True)


def student_call(feats, protos, part, parts, after=(), size=512, chunk=1024):
    rows, width = feats.shape
    count = protos.shape[1] // parts
    return pl.pallas_call(
        functools.partial(student_kernel, size=size, chunk=chunk, start=part * count),
        in_specs=[WHOLE, ANY] + [ANY] * len(after),
        out_specs=[WHOLE] * 3,
        out_shape=[
            jax.ShapeDtypeStruct((rows, width), F32),
            pltpu.VMEM((width, count), BF16),
            jax.ShapeDtypeStruct((1, rows), F32),
        ],
        scratch_shapes=[pltpu.VMEM((width, count), BF16), pltpu.SemaphoreType.DMA((count // chunk,))],
        compiler_params=params(10),
        cost_estimate=cost(2.0),
        name="student",
    )(feats, in_hbm(protos), *after)


def tall_kernel(place, protos, *refs, pieces, turn, made, scale, size=512):
    outs = refs[len(refs) - 2 - (1 + turn + made) : len(refs) - 2]
    energy = outs[0]
    held, arrived = refs[-2:]
    rows = refs[0].shape[0]
    width, count = held.shape
    if made:
        (copy,) = fetch(protos, held, arrived, count, pl.multiple_of(place[0] * count, count))
    side = slice(width, 2 * width) if turn else slice(0, width)
    feats = [refs[k][:, side] for k in range(pieces)]
    if turn:
        for k in range(pieces):
            outs[1][:, k * rows : (k + 1) * rows] = feats[k].T.astype(BF16)
    feats = [value.astype(BF16) for value in feats]
    for at in range(0, count, size):
        here = slice(at, at + size)
        if made:
            if at == 0:
                copy.wait()
            unit, _ = unit_columns(held[:, here])
            outs[-1][:, here] = unit
        else:
            unit = refs[pieces][:, here]
        for k in range(pieces):
            score = jnp.dot(feats[k], unit, preferred_element_type=F32)
            energy[k * rows : (k + 1) * rows, here] = jnp.exp2(score * (scale * LOG2E)).astype(BF16)


def tall_call(place, protos, feats, turn, scale, name, unit=None, after=(), size=512):
    rows = feats[0].shape[0] * len(feats)
    width, count = protos.shape
    count = count // 4
    made = unit is None
    out_shape = [pltpu.VMEM((rows, count), BF16)]
    if turn:
        out_shape.append(jax.ShapeDtypeStruct((width, rows), BF16))
    if made:
        out_shape.append(pltpu.VMEM((width, count), BF16))
    given = [] if made else [in_vmem(unit)]
    return pl.pallas_call(
        functools.partial(tall_kernel, pieces=len(feats), turn=turn, made=made, scale=scale, size=size),
        in_specs=[SCALARS, ANY] + [WHOLE] * (len(feats) + len(given)) + [ANY] * len(after),
        out_specs=[WHOLE] * len(out_shape),
        out_shape=out_shape,
        scratch_shapes=[pltpu.VMEM((width, count), BF16), pltpu.SemaphoreType.DMA((1,))],
        compiler_params=params(10),
        cost_estimate=cost(2.5),
        name=name,
    )(place, in_hbm(protos), *feats, *given, *after)


def row_kernel(energy, col_total, *refs, total_protos, size=512):
    row_part, lanes, scales = refs[-3:]
    rows, count = energy.shape
    cut = count // 2
    scales[...] = jnp.broadcast_to(1.0 / (total_protos * col_total[:, cut:]), scales.shape)
    total = jnp.zeros((16, rows), F32)
    steps = cut // size
    groups = rows // 16 // steps
    for step in range(steps):
        at = step * size
        scale = two_terms(1.0 / (total_protos * col_total[:, at : at + size]))
        total = total + lax.dot_general(
            scale, energy[:, at : at + size], (((1,), (1,)), ((), ())), preferred_element_type=F32
        )
        for group in range(step * groups, (step + 1) * groups):
            here = slice(group * 16, (group + 1) * 16)
            sums = [jnp.zeros((16, 128), F32)] * 2
            for tile in range((count - cut) // 128):
                lane = slice(tile * 128, (tile + 1) * 128)
                value = energy[here, cut + tile * 128 : cut + (tile + 1) * 128].astype(F32)
                sums[tile % 2] = sums[tile % 2] + value * scales[:, lane]
            lanes[here, :] = sums[0] + sums[1]
    row_part[...] = jnp.sum(total, axis=0, keepdims=True) + jnp.sum(lanes[...].T, axis=0, keepdims=True)


def row_call(energy, col_total, total_protos, after=()):
    rows, count = energy.shape
    return pl.pallas_call(
        functools.partial(row_kernel, total_protos=total_protos),
        in_specs=[WHOLE, WHOLE] + [ANY] * len(after),
        out_specs=WHOLE,
        out_shape=jax.ShapeDtypeStruct((1, rows), F32),
        scratch_shapes=[pltpu.VMEM((rows, 128), F32), pltpu.VMEM((16, count // 2), F32)],
        compiler_params=params(6),
        name="row_pass",
    )(in_vmem(energy), col_total, *after)


def col_kernel(energy, row_total, *refs, total_rows, size=1024):
    col_part = refs[-1]
    scale = two_terms(1.0 / (total_rows * row_total[...]))
    for at in range(0, energy.shape[1], size):
        part = jnp.dot(scale, energy[:, at : at + size], preferred_element_type=F32)
        col_part[:, at : at + size] = jnp.sum(part, axis=0, keepdims=True)


def col_call(energy, row_total, total_rows, after=()):
    return pl.pallas_call(
        functools.partial(col_kernel, total_rows=total_rows),
        in_specs=[WHOLE, WHOLE] + [ANY] * len(after),
        out_specs=WHOLE,
        out_shape=jax.ShapeDtypeStruct((1, energy.shape[1]), F32),
        compiler_params=params(4),
        name="col_pass",
    )(in_vmem(energy), row_total, *after)


def target_kernel(energy, col_total, *refs, parts, total_protos, size):
    unit = refs[:parts]
    feat_part = refs[-1]
    places = [(part, at) for part in unit for at in range(0, part.shape[1], size)]
    for at, (part_of, start) in zip(range(0, energy.shape[1], size), places):
        here = slice(start, start + size)
        scale = 1.0 / (total_protos * col_total[:, at : at + size])
        scaled = (part_of[:, here].astype(F32) * scale).astype(BF16)
        part = lax.dot_general(energy[:, at : at + size], scaled, (((1,), (1,)), ((), ())), preferred_element_type=F32)
        feat_part[...] = feat_part[...] + part if at else part


def target_call(energy, unit, col_total, total_protos, after=(), size=1024):
    parts = len(unit)
    return pl.pallas_call(
        functools.partial(target_kernel, parts=parts, total_protos=total_protos, size=size),
        in_specs=[WHOLE] * (2 + parts) + [ANY] * len(after),
        out_specs=WHOLE,
        out_shape=jax.ShapeDtypeStruct((energy.shape[0], unit[0].shape[0]), F32),
        compiler_params=params(10),
        cost_estimate=cost(3.0),
        name="feat_target",
    )(in_vmem(energy), col_total, *[in_vmem(part) for part in unit], *after)


def mix_kernel(place, target, totals, *refs, parts):
    prob = refs[:parts]
    mine, other, total = refs[-3:]
    wide = target.shape[1] // 128
    rows_r = jnp.concatenate([across(STUDENT_SCALE / totals[:1, :])] * wide, axis=1)
    rows_s = jnp.concatenate([across(STUDENT_SCALE / totals[1:, :])] * wide, axis=1)
    whole = prob[0][...]
    for part in prob[1:]:
        whole = whole + part[...]
    total[...] = whole * rows_s - target[...] * rows_r
    rows = mine.shape[0]
    mine[...] = total[pl.ds(pl.multiple_of(place[1] * rows, rows), rows), :]
    other[...] = total[pl.ds(pl.multiple_of((1 - place[1]) * rows, rows), rows), :]


def mix_call(place, target, totals, prob):
    rows, width = target.shape
    return pl.pallas_call(
        functools.partial(mix_kernel, parts=len(prob)),
        in_specs=[SCALARS] + [WHOLE] * (2 + len(prob)),
        out_specs=[WHOLE] * 2,
        out_shape=[jax.ShapeDtypeStruct((rows // 2, width), F32)] * 2,
        scratch_shapes=[pltpu.VMEM((rows, width), F32)],
        compiler_params=params(10),
        cost_estimate=cost(1.0),
        name="feat_mix",
    )(place, target, totals, *prob)


def proto_kernel(place, protos, col_total, *refs, pieces, total_protos, size):
    energy, expo, turned, totals = refs[:2], refs[2:4], refs[4:6], refs[6 : 6 + pieces]
    grad, held, made, row_scale, soft_scale, arrived, left = refs[-7:]
    width, count = held.shape
    first = pl.multiple_of(place[0] * count, count)
    (copy,) = fetch(protos, held, arrived, count, first)
    tall = energy[0].shape[0]
    rows = tall // pieces
    for k in range(pieces):
        for half in range(2):
            side = jnp.where(place[1] == half, 0, 1)
            turn = (pieces - k) % pieces if half else k
            there = pl.ds(pl.multiple_of(side * tall + turn * rows, rows), rows)
            own = STUDENT_SCALE / totals[k][:, half * rows : (half + 1) * rows]
            row_scale[:, there] = own[:1]
            soft_scale[:, there] = own[1:]
    scaled = []
    for side in range(2):
        there = slice(side * tall, (side + 1) * tall)
        wide = turned[side][...].astype(F32)
        scaled.append(((wide * row_scale[:, there]).astype(BF16), (wide * soft_scale[:, there]).astype(BF16)))
    copies = []
    for at in range(0, count, size):
        here = slice(at, at + size)
        scale = 1.0 / (total_protos * col_total[:, pl.ds(first + at, size)])
        target = jnp.dot(scaled[0][0], energy[0][:, here], preferred_element_type=F32)
        target = target + jnp.dot(scaled[1][0], energy[1][:, here], preferred_element_type=F32)
        part = jnp.dot(scaled[0][1], expo[0][:, here], preferred_element_type=F32)
        part = part + jnp.dot(scaled[1][1], expo[1][:, here], preferred_element_type=F32)
        part = part - target * scale
        if at == 0:
            copy.wait()
        unit, norm = unit_columns(held[:, here])
        wide_unit = unit.astype(F32)
        dots = jnp.sum(wide_unit * part, axis=0, keepdims=True)
        made[:, here] = (part - wide_unit * dots) * (1.0 / norm)
        copies.append(pltpu.make_async_copy(made.at[:, here], grad.at[:, here], left.at[at // size]))
        copies[-1].start()
    for copy in copies:
        copy.wait()


def proto_call(place, protos, energy, expo, turned, col_total, totals, total_protos, after=(), size=512):
    rows, count = energy[0].shape
    width = protos.shape[0]
    return pl.pallas_call(
        functools.partial(proto_kernel, pieces=len(totals), total_protos=total_protos, size=size),
        in_specs=[SCALARS, ANY] + [WHOLE] * (7 + len(totals)) + [ANY] * len(after),
        out_specs=ANY,
        out_shape=pltpu.HBM((width, count), F32),
        scratch_shapes=[
            pltpu.VMEM((width, count), BF16),
            pltpu.VMEM((width, count), F32),
            pltpu.VMEM((1, 2 * rows), F32),
            pltpu.VMEM((1, 2 * rows), F32),
            pltpu.SemaphoreType.DMA((1,)),
            pltpu.SemaphoreType.DMA((count // size,)),
        ],
        compiler_params=params(20),
        cost_estimate=cost(8.0),
        name="proto_grad",
    )(
        place, in_hbm(protos), col_total, *[in_vmem(part) for part in energy], *[in_vmem(part) for part in expo],
        *turned, *totals, *after,
    )


def finish_kernel(place, feats, first, second, third, fourth, grad):
    rows = grad.shape[0]
    here = pl.ds(pl.multiple_of(place[1] * rows, rows), rows)
    unit, norm = unit_rows(feats[here, :])
    unit = unit.astype(F32)
    feat_sum = (first[...] + second[...]) + (third[...] + fourth[...])
    along = jnp.sum(unit * feat_sum, axis=1, keepdims=True)
    grad[...] = (feat_sum - unit * along) / norm


def finish_call(place, feats, parts):
    return pl.pallas_call(
        finish_kernel,
        in_specs=[SCALARS] + [WHOLE] * (1 + len(parts)),
        out_specs=WHOLE,
        out_shape=jax.ShapeDtypeStruct(parts[0].shape, F32),
        compiler_params=params(8),
        cost_estimate=cost(1.0),
        name="finish",
    )(place, feats, *parts)


def join_kernel(place, mine, other, whole):
    rows = mine.shape[0]
    whole[pl.ds(pl.multiple_of(place[1] * rows, rows), rows), :] = mine[...]
    whole[pl.ds(pl.multiple_of((1 - place[1]) * rows, rows), rows), :] = other[...]


def join_call(place, mine, other):
    rows, width = mine.shape
    return pl.pallas_call(
        join_kernel,
        in_specs=[SCALARS, WHOLE, WHOLE],
        out_specs=WHOLE,
        out_shape=jax.ShapeDtypeStruct((2 * rows, width), F32),
        compiler_params=params(8),
        cost_estimate=cost(1.0),
        name="join",
    )(place, mine, other)


def shifted(value, axis, shift):
    size = SIZES[axis]
    return lax.ppermute(value, axis, [(i, (i + shift) % size) for i in range(size)])


def two_way(value):
    pairs = []
    for z in range(4):
        pairs.append((2 * z, 2 * ((z + 1) % 4)))
        pairs.append((2 * z + 1, 2 * ((z + 3) % 4) + 1))
    return lax.ppermute(value, ("z", "core"), pairs)


def ring_parts(value, axis):
    made = {shift: shifted(value, axis, shift) for shift in ((1, 3, 2) if SIZES[axis] == 4 else (1,))}
    return [value] + [made[shift] for shift in sorted(made)]


def ring_sum(value, axis):
    parts = ring_parts(value, axis)
    value = parts[0]
    for part in parts[1:]:
        value = value + part
    return value


def batch_sum(value):
    return ring_sum(ring_sum(value, "x"), "z")


def x_sum(value, after):
    return add_call(ring_parts(value, "x"), after)


def proto_sum(value):
    return ring_sum(ring_sum(value, "core"), "y")


def on_device(student_feats, teacher_feats, protos, teacher_protos):
    rows, width = student_feats.shape
    count = protos.shape[1]
    total_rows = rows * 16
    total_protos = count * 8
    place = jnp.stack([lax.axis_index("z"), lax.axis_index("core")]).astype(jnp.int32)

    near, far = units_call(place, teacher_feats, student_feats)
    first = two_way(near)
    energy, col_part = energy_call(place, teacher_feats, teacher_protos)
    col_total = batch_sum(col_part)
    second = two_way(first)
    students = [student_call(student_feats, protos, 0, 2, (col_part,))]
    row_part = row_call(energy, col_total, total_protos, (students[0][2], first))
    students.append(student_call(student_feats, protos, 2, 4, (row_part,)))
    row_total = proto_sum(row_part)
    third = two_way(second)
    col_part = col_call(energy, row_total, total_rows, (second, students[1][2]))
    students.append(student_call(student_feats, protos, 3, 4, (col_part,)))
    soft_part = students[0][2] + students[1][2] + students[2][2]
    col_total = batch_sum(col_part)
    row_part = row_call(energy, col_total, total_protos, (third, students[2][2]))
    near_side = [near, first, second, third]
    far_side = [far] + [shifted(part, "core", 1) for part in (first, second, third)]
    row_total = proto_sum(row_part)
    near_expo, near_turned, student_columns = tall_call(
        place, protos, near_side, 1, STUDENT_SCALE, "tall_expo", None, (row_part,)
    )
    col_part = col_call(energy, row_total, total_rows, (near_turned,))
    far_expo, far_turned = tall_call(
        place, protos, far_side, 1, STUDENT_SCALE, "tall_expo", student_columns, (col_part,)
    )
    col_half = x_sum(col_part, (far_turned,))
    near_energy, teacher_columns = tall_call(
        place, teacher_protos, near_side, 0, TEACHER_SCALE, "tall_energy", None, (col_half,)
    )
    col_total = ring_sum(col_half, "z")
    row_part = row_call(energy, col_total, total_protos, (near_energy,))
    feat_target = target_call(energy, [made[1] for made in students], col_total, total_protos, (row_part,))
    totals = proto_sum(jnp.concatenate([row_part, soft_part], axis=0))
    mine, other = mix_call(place, feat_target, totals, [made[0] for made in students])
    feat_half = mine + shifted(other, "core", 1)
    (far_energy,) = tall_call(
        place, teacher_protos, far_side, 0, TEACHER_SCALE, "tall_energy", teacher_columns, (totals,)
    )
    grad_part = proto_call(
        place, protos, [near_energy, far_energy], [near_expo, far_expo], [near_turned, far_turned], col_total,
        ring_parts(totals, "z"), total_protos, (feat_half,),
    )
    pieces = lax.all_to_all(grad_part.reshape(16, width // 16, count // 4), BATCH, 0, 0)
    pieces = jnp.sum(pieces.reshape(4, 4, width // 16, count // 4), axis=0)
    grad_protos = pieces.transpose(1, 0, 2).reshape(width // 16, count)

    grad_half = finish_call(place, student_feats, ring_parts(feat_half, "y"))
    return join_call(place, grad_half, shifted(grad_half, "core", 1)), grad_protos


def solution(mesh):
    split = Mesh(mesh.devices.reshape(4, 4, 4, 2), ("x", "z", "y", "core"))
    return jax.shard_map(
        on_device,
        mesh=split,
        in_specs=(P(BATCH, None), P(BATCH, None), P(None, PROTO), P(None, PROTO)),
        out_specs=(P(BATCH, None), P(BATCH, PROTO)),
        check_vma=False,
    )
```

```python
import functools

import jax
import jax.numpy as jnp
from jax import lax
from jax.experimental import pallas as pl
from jax.experimental.pallas import tpu as pltpu
from jax.sharding import Mesh
from jax.sharding import PartitionSpec as P

EPSILON = 1e-06
TEACHER_SCALE = 25.0
STUDENT_SCALE = 10.0
LOG2E = 1.4426950408889634
SIZES = {"x": 4, "z": 4, "y": 4, "core": 2}
BATCH = ("x", "z")
PROTO = ("y", "core")
WHOLE = pl.BlockSpec(memory_space=pltpu.VMEM)
SCALARS = pl.BlockSpec(memory_space=pltpu.SMEM)
ANY = pl.BlockSpec(memory_space=pl.ANY)
F32 = jnp.float32
BF16 = jnp.bfloat16


def params(mib):
    return pltpu.CompilerParams(vmem_limit_bytes=mib << 20)


def cost(microseconds):
    return pl.CostEstimate(flops=0, bytes_accessed=int(microseconds * 3.0e6), transcendentals=0)


def in_vmem(value):
    return pltpu.with_memory_space_constraint(value, pltpu.VMEM)


def in_hbm(value):
    return pltpu.with_memory_space_constraint(value, pltpu.HBM)


def unit_rows(values):
    wide = values.astype(F32)
    norms = jnp.sqrt(jnp.sum(wide * wide, axis=1, keepdims=True) + EPSILON)
    return (wide / norms).astype(BF16), norms


def unit_columns(values):
    wide = values.astype(F32)
    norms = jnp.sqrt(jnp.sum(wide * wide, axis=0, keepdims=True) + EPSILON)
    return (wide * (1.0 / norms)).astype(BF16), norms


def across(row, lanes=128):
    return jnp.broadcast_to(row, (lanes, row.shape[1])).T


def two_terms(row):
    high = row.astype(BF16).astype(F32)
    place = lax.broadcasted_iota(jnp.int32, (16, row.shape[1]), 0)
    return jnp.where(place == 0, high, jnp.where(place == 1, row - high, 0.0)).astype(BF16)


def fetch(source, held, arrived, chunk, start=0):
    copies = [
        pltpu.make_async_copy(
            source.at[:, pl.ds(start + at, chunk)], held.at[:, at : at + chunk], arrived.at[at // chunk]
        )
        for at in range(0, held.shape[1], chunk)
    ]
    for copy in copies:
        copy.start()
    return copies


def energy_kernel(place, feats, protos, *refs, size, chunk):
    energy, col_sum, held, arrived = refs[-4:]
    copies = fetch(protos, held, arrived, chunk)
    teacher, _ = unit_rows(feats[...])
    for at in range(0, held.shape[1], size):
        if at % chunk == 0:
            copies[at // chunk].wait()
        unit, _ = unit_columns(held[:, at : at + size])
        score = jnp.dot(teacher, unit, preferred_element_type=F32)
        value = jnp.exp2(score * (TEACHER_SCALE * LOG2E))
        energy[:, at : at + size] = value.astype(BF16)
        col_sum[:, at : at + size] = jnp.sum(value, axis=0, keepdims=True)


def energy_call(place, feats, protos, after=(), size=512, chunk=2048):
    rows, width = feats.shape
    count = protos.shape[1]
    return pl.pallas_call(
        functools.partial(energy_kernel, size=size, chunk=chunk),
        in_specs=[SCALARS, WHOLE, ANY] + [ANY] * len(after),
        out_specs=[WHOLE, WHOLE],
        out_shape=[pltpu.VMEM((rows, count), BF16), jax.ShapeDtypeStruct((1, count), F32)],
        scratch_shapes=[pltpu.VMEM((width, count), BF16), pltpu.SemaphoreType.DMA((count // chunk,))],
        compiler_params=params(10),
        cost_estimate=cost(5.0),
        name="energy",
    )(place, in_hbm(feats), in_hbm(protos), *after)


def units_kernel(place, teacher, student, *refs):
    mine, other = refs[-2:]
    rows, width = mine.shape
    for side, target in ((place[1], mine), (1 - place[1], other)):
        here = pl.ds(pl.multiple_of(side * rows, rows), rows)
        target[:, : width // 2] = unit_rows(teacher[here, :])[0].astype(F32)
        target[:, width // 2 :] = unit_rows(student[here, :])[0].astype(F32)


def units_call(place, teacher, student, after=()):
    rows, width = teacher.shape
    return pl.pallas_call(
        units_kernel,
        in_specs=[SCALARS, WHOLE, WHOLE] + [ANY] * len(after),
        out_specs=[WHOLE] * 2,
        out_shape=[jax.ShapeDtypeStruct((rows // 2, 2 * width), F32)] * 2,
        compiler_params=params(8),
        cost_estimate=cost(1.5),
        name="units",
    )(place, teacher, student, *after)


def add_kernel(first, second, third, fourth, *refs):
    refs[-1][...] = (first[...] + second[...]) + (third[...] + fourth[...])


def add_call(parts, after):
    return pl.pallas_call(
        add_kernel,
        in_specs=[WHOLE] * 4 + [ANY] * len(after),
        out_specs=WHOLE,
        out_shape=jax.ShapeDtypeStruct(parts[0].shape, F32),
        compiler_params=params(4),
        cost_estimate=cost(0.5),
        name="add",
    )(*parts, *after)


def student_kernel(feats, protos, *refs, size, chunk, start):
    feat_part, unit_out, row_sum, held, arrived = refs[-5:]
    copies = fetch(protos, held, arrived, chunk, start)
    student, _ = unit_rows(feats[...])
    total = jnp.zeros((feats.shape[0], 128), F32)
    for at in range(0, held.shape[1], size):
        if at % chunk == 0:
            copies[at // chunk].wait()
        unit, _ = unit_columns(held[:, at : at + size])
        unit_out[:, at : at + size] = unit
        score = jnp.dot(student, unit, preferred_element_type=F32)
        value = jnp.exp2(score * (STUDENT_SCALE * LOG2E))
        part = lax.dot_general(value.astype(BF16), unit, (((1,), (1,)), ((), ())), preferred_element_type=F32)
        feat_part[...] = feat_part[...] + part if at else part
        for tile in range(0, size, 128):
            total = total + value[:, tile : tile + 128]
    row_sum[...] = jnp.sum(total.T, axis=0, keepdims=True)


def student_call(feats, protos, part, parts, after=(), size=512, chunk=1024):
    rows, width = feats.shape
    count = protos.shape[1] // parts
    return pl.pallas_call(
        functools.partial(student_kernel, size=size, chunk=chunk, start=part * count),
        in_specs=[WHOLE, ANY] + [ANY] * len(after),
        out_specs=[WHOLE] * 3,
        out_shape=[
            jax.ShapeDtypeStruct((rows, width), F32),
            pltpu.VMEM((width, count), BF16),
            jax.ShapeDtypeStruct((1, rows), F32),
        ],
        scratch_shapes=[pltpu.VMEM((width, count), BF16), pltpu.SemaphoreType.DMA((count // chunk,))],
        compiler_params=params(10),
        cost_estimate=cost(2.0),
        name="student",
    )(feats, in_hbm(protos), *after)


def tall_kernel(place, protos, *refs, pieces, turn, made, scale, size=512):
    outs = refs[len(refs) - 2 - (1 + turn + 2 * made) : len(refs) - 2]
    energy = outs[0]
    held, arrived = refs[-2:]
    rows = refs[0].shape[0]
    width, count = held.shape
    if made:
        (copy,) = fetch(protos, held, arrived, count, pl.multiple_of(place[0] * count, count))
    side = slice(width, 2 * width) if turn else slice(0, width)
    feats = [refs[k][:, side] for k in range(pieces)]
    if turn:
        for k in range(pieces):
            outs[1][:, k * rows : (k + 1) * rows] = feats[k].T.astype(BF16)
    feats = [value.astype(BF16) for value in feats]
    for at in range(0, count, size):
        here = slice(at, at + size)
        if made:
            if at == 0:
                copy.wait()
            unit, norm = unit_columns(held[:, here])
            outs[-2][:, here] = unit
            outs[-1][:, here] = 1.0 / norm
        else:
            unit = refs[pieces][:, here]
        for k in range(pieces):
            score = jnp.dot(feats[k], unit, preferred_element_type=F32)
            energy[k * rows : (k + 1) * rows, here] = jnp.exp2(score * (scale * LOG2E)).astype(BF16)


def tall_call(place, protos, feats, turn, scale, name, unit=None, after=(), size=512):
    rows = feats[0].shape[0] * len(feats)
    width, count = protos.shape
    count = count // 4
    made = unit is None
    out_shape = [pltpu.VMEM((rows, count), BF16)]
    if turn:
        out_shape.append(jax.ShapeDtypeStruct((width, rows), BF16))
    if made:
        out_shape.append(pltpu.VMEM((width, count), BF16))
        out_shape.append(jax.ShapeDtypeStruct((1, count), F32))
    given = [] if made else [in_vmem(unit)]
    return pl.pallas_call(
        functools.partial(tall_kernel, pieces=len(feats), turn=turn, made=made, scale=scale, size=size),
        in_specs=[SCALARS, ANY] + [WHOLE] * (len(feats) + len(given)) + [ANY] * len(after),
        out_specs=[WHOLE] * len(out_shape),
        out_shape=out_shape,
        scratch_shapes=[pltpu.VMEM((width, count), BF16), pltpu.SemaphoreType.DMA((1,))],
        compiler_params=params(10),
        cost_estimate=cost(2.5),
        name=name,
    )(place, in_hbm(protos), *feats, *given, *after)


def row_kernel(energy, col_total, *refs, total_protos, size=512):
    row_part, lanes, scales = refs[-3:]
    rows, count = energy.shape
    cut = count // 2
    scales[...] = jnp.broadcast_to(1.0 / (total_protos * col_total[:, cut:]), scales.shape)
    total = jnp.zeros((16, rows), F32)
    steps = cut // size
    groups = rows // 16 // steps
    for step in range(steps):
        at = step * size
        scale = two_terms(1.0 / (total_protos * col_total[:, at : at + size]))
        total = total + lax.dot_general(
            scale, energy[:, at : at + size], (((1,), (1,)), ((), ())), preferred_element_type=F32
        )
        for group in range(step * groups, (step + 1) * groups):
            here = slice(group * 16, (group + 1) * 16)
            sums = [jnp.zeros((16, 128), F32)] * 2
            for tile in range((count - cut) // 128):
                lane = slice(tile * 128, (tile + 1) * 128)
                value = energy[here, cut + tile * 128 : cut + (tile + 1) * 128].astype(F32)
                sums[tile % 2] = sums[tile % 2] + value * scales[:, lane]
            lanes[here, :] = sums[0] + sums[1]
    row_part[...] = jnp.sum(total, axis=0, keepdims=True) + jnp.sum(lanes[...].T, axis=0, keepdims=True)


def row_call(energy, col_total, total_protos, after=()):
    rows, count = energy.shape
    return pl.pallas_call(
        functools.partial(row_kernel, total_protos=total_protos),
        in_specs=[WHOLE, WHOLE] + [ANY] * len(after),
        out_specs=WHOLE,
        out_shape=jax.ShapeDtypeStruct((1, rows), F32),
        scratch_shapes=[pltpu.VMEM((rows, 128), F32), pltpu.VMEM((16, count // 2), F32)],
        compiler_params=params(6),
        name="row_pass",
    )(in_vmem(energy), col_total, *after)


def col_kernel(energy, row_total, *refs, total_rows, size=1024):
    col_part = refs[-1]
    scale = two_terms(1.0 / (total_rows * row_total[...]))
    for at in range(0, energy.shape[1], size):
        part = jnp.dot(scale, energy[:, at : at + size], preferred_element_type=F32)
        col_part[:, at : at + size] = jnp.sum(part, axis=0, keepdims=True)


def col_call(energy, row_total, total_rows, after=()):
    return pl.pallas_call(
        functools.partial(col_kernel, total_rows=total_rows),
        in_specs=[WHOLE, WHOLE] + [ANY] * len(after),
        out_specs=WHOLE,
        out_shape=jax.ShapeDtypeStruct((1, energy.shape[1]), F32),
        compiler_params=params(4),
        name="col_pass",
    )(in_vmem(energy), row_total, *after)


def target_kernel(energy, col_total, *refs, parts, total_protos, size):
    unit = refs[:parts]
    feat_part = refs[-1]
    places = [(part, at) for part in unit for at in range(0, part.shape[1], size)]
    for at, (part_of, start) in zip(range(0, energy.shape[1], size), places):
        here = slice(start, start + size)
        scale = 1.0 / (total_protos * col_total[:, at : at + size])
        scaled = (part_of[:, here].astype(F32) * scale).astype(BF16)
        part = lax.dot_general(energy[:, at : at + size], scaled, (((1,), (1,)), ((), ())), preferred_element_type=F32)
        feat_part[...] = feat_part[...] + part if at else part


def target_call(energy, unit, col_total, total_protos, after=(), size=1024):
    parts = len(unit)
    return pl.pallas_call(
        functools.partial(target_kernel, parts=parts, total_protos=total_protos, size=size),
        in_specs=[WHOLE] * (2 + parts) + [ANY] * len(after),
        out_specs=WHOLE,
        out_shape=jax.ShapeDtypeStruct((energy.shape[0], unit[0].shape[0]), F32),
        compiler_params=params(10),
        cost_estimate=cost(3.0),
        name="feat_target",
    )(in_vmem(energy), col_total, *[in_vmem(part) for part in unit], *after)


def mix_kernel(place, target, totals, *refs, parts):
    prob = refs[:parts]
    mine, other, total = refs[-3:]
    wide = target.shape[1] // 128
    rows_r = jnp.concatenate([across(STUDENT_SCALE / totals[:1, :])] * wide, axis=1)
    rows_s = jnp.concatenate([across(STUDENT_SCALE / totals[1:, :])] * wide, axis=1)
    whole = prob[0][...]
    for part in prob[1:]:
        whole = whole + part[...]
    total[...] = whole * rows_s - target[...] * rows_r
    rows = mine.shape[0]
    mine[...] = total[pl.ds(pl.multiple_of(place[1] * rows, rows), rows), :]
    other[...] = total[pl.ds(pl.multiple_of((1 - place[1]) * rows, rows), rows), :]


def mix_call(place, target, totals, prob):
    rows, width = target.shape
    return pl.pallas_call(
        functools.partial(mix_kernel, parts=len(prob)),
        in_specs=[SCALARS] + [WHOLE] * (2 + len(prob)),
        out_specs=[WHOLE] * 2,
        out_shape=[jax.ShapeDtypeStruct((rows // 2, width), F32)] * 2,
        scratch_shapes=[pltpu.VMEM((rows, width), F32)],
        compiler_params=params(10),
        cost_estimate=cost(1.0),
        name="feat_mix",
    )(place, target, totals, *prob)


def proto_kernel(place, unit, scale_out, col_total, *refs, pieces, total_protos, size):
    energy, expo, turned, totals = refs[:2], refs[2:4], refs[4:6], refs[6 : 6 + pieces]
    grad, made, row_scale, soft_scale, left = refs[-5:]
    width, count = unit.shape
    first = pl.multiple_of(place[0] * count, count)
    tall = energy[0].shape[0]
    rows = tall // pieces
    for k in range(pieces):
        for half in range(2):
            side = jnp.where(place[1] == half, 0, 1)
            turn = (pieces - k) % pieces if half else k
            there = pl.ds(pl.multiple_of(side * tall + turn * rows, rows), rows)
            own = STUDENT_SCALE / totals[k][:, half * rows : (half + 1) * rows]
            row_scale[:, there] = own[:1]
            soft_scale[:, there] = own[1:]
    scaled = []
    for side in range(2):
        there = slice(side * tall, (side + 1) * tall)
        wide = turned[side][...].astype(F32)
        scaled.append(((wide * row_scale[:, there]).astype(BF16), (wide * soft_scale[:, there]).astype(BF16)))
    copies = []
    for at in range(0, count, size):
        here = slice(at, at + size)
        scale = 1.0 / (total_protos * col_total[:, pl.ds(first + at, size)])
        target = jnp.dot(scaled[0][0], energy[0][:, here], preferred_element_type=F32)
        target = target + jnp.dot(scaled[1][0], energy[1][:, here], preferred_element_type=F32)
        part = jnp.dot(scaled[0][1], expo[0][:, here], preferred_element_type=F32)
        part = part + jnp.dot(scaled[1][1], expo[1][:, here], preferred_element_type=F32)
        part = part - target * scale
        wide_unit = unit[:, here].astype(F32)
        dots = jnp.sum(wide_unit * part, axis=0, keepdims=True)
        made[:, here] = (part - wide_unit * dots) * scale_out[:, here]
        copies.append(pltpu.make_async_copy(made.at[:, here], grad.at[:, here], left.at[at // size]))
        copies[-1].start()
    for copy in copies:
        copy.wait()


def proto_call(place, unit, scale_out, energy, expo, turned, col_total, totals, total_protos, after=(), size=512):
    rows, count = energy[0].shape
    width = unit.shape[0]
    return pl.pallas_call(
        functools.partial(proto_kernel, pieces=len(totals), total_protos=total_protos, size=size),
        in_specs=[SCALARS] + [WHOLE] * (9 + len(totals)) + [ANY] * len(after),
        out_specs=ANY,
        out_shape=pltpu.HBM((width, count), F32),
        scratch_shapes=[
            pltpu.VMEM((width, count), F32),
            pltpu.VMEM((1, 2 * rows), F32),
            pltpu.VMEM((1, 2 * rows), F32),
            pltpu.SemaphoreType.DMA((count // size,)),
        ],
        compiler_params=params(20),
        cost_estimate=cost(8.0),
        name="proto_grad",
    )(
        place, in_vmem(unit), scale_out, col_total, *[in_vmem(part) for part in energy], *[in_vmem(part) for part in expo],
        *turned, *totals, *after,
    )


def finish_kernel(place, feats, first, second, third, fourth, grad):
    rows = grad.shape[0]
    here = pl.ds(pl.multiple_of(place[1] * rows, rows), rows)
    unit, norm = unit_rows(feats[here, :])
    unit = unit.astype(F32)
    feat_sum = (first[...] + second[...]) + (third[...] + fourth[...])
    along = jnp.sum(unit * feat_sum, axis=1, keepdims=True)
    grad[...] = (feat_sum - unit * along) / norm


def finish_call(place, feats, parts):
    return pl.pallas_call(
        finish_kernel,
        in_specs=[SCALARS] + [WHOLE] * (1 + len(parts)),
        out_specs=WHOLE,
        out_shape=jax.ShapeDtypeStruct(parts[0].shape, F32),
        compiler_params=params(8),
        cost_estimate=cost(1.0),
        name="finish",
    )(place, feats, *parts)


def join_kernel(place, mine, other, whole):
    rows = mine.shape[0]
    whole[pl.ds(pl.multiple_of(place[1] * rows, rows), rows), :] = mine[...]
    whole[pl.ds(pl.multiple_of((1 - place[1]) * rows, rows), rows), :] = other[...]


def join_call(place, mine, other):
    rows, width = mine.shape
    return pl.pallas_call(
        join_kernel,
        in_specs=[SCALARS, WHOLE, WHOLE],
        out_specs=WHOLE,
        out_shape=jax.ShapeDtypeStruct((2 * rows, width), F32),
        compiler_params=params(8),
        cost_estimate=cost(1.0),
        name="join",
    )(place, mine, other)


def shifted(value, axis, shift):
    size = SIZES[axis]
    return lax.ppermute(value, axis, [(i, (i + shift) % size) for i in range(size)])


def two_way(value):
    pairs = []
    for z in range(4):
        pairs.append((2 * z, 2 * ((z + 1) % 4)))
        pairs.append((2 * z + 1, 2 * ((z + 3) % 4) + 1))
    return lax.ppermute(value, ("z", "core"), pairs)


def ring_parts(value, axis):
    made = {shift: shifted(value, axis, shift) for shift in ((1, 3, 2) if SIZES[axis] == 4 else (1,))}
    return [value] + [made[shift] for shift in sorted(made)]


def ring_sum(value, axis):
    parts = ring_parts(value, axis)
    value = parts[0]
    for part in parts[1:]:
        value = value + part
    return value


def batch_sum(value):
    return ring_sum(ring_sum(value, "x"), "z")


def x_sum(value, after):
    return add_call(ring_parts(value, "x"), after)


def proto_sum(value):
    return ring_sum(ring_sum(value, "core"), "y")


def on_device(student_feats, teacher_feats, protos, teacher_protos):
    rows, width = student_feats.shape
    count = protos.shape[1]
    total_rows = rows * 16
    total_protos = count * 8
    place = jnp.stack([lax.axis_index("z"), lax.axis_index("core")]).astype(jnp.int32)

    near, far = units_call(place, teacher_feats, student_feats)
    first = two_way(near)
    energy, col_part = energy_call(place, teacher_feats, teacher_protos)
    col_total = batch_sum(col_part)
    second = two_way(first)
    students = [student_call(student_feats, protos, 0, 2, (col_part,))]
    row_part = row_call(energy, col_total, total_protos, (students[0][2], first))
    students.append(student_call(student_feats, protos, 2, 4, (row_part,)))
    row_total = proto_sum(row_part)
    third = two_way(second)
    col_part = col_call(energy, row_total, total_rows, (second, students[1][2]))
    students.append(student_call(student_feats, protos, 3, 4, (col_part,)))
    soft_part = students[0][2] + students[1][2] + students[2][2]
    col_total = batch_sum(col_part)
    row_part = row_call(energy, col_total, total_protos, (third, students[2][2]))
    near_side = [near, first, second, third]
    far_side = [far] + [shifted(part, "core", 1) for part in (first, second, third)]
    row_total = proto_sum(row_part)
    near_expo, near_turned, student_columns, scale_out = tall_call(
        place, protos, near_side, 1, STUDENT_SCALE, "tall_expo", None, (row_part,)
    )
    col_part = col_call(energy, row_total, total_rows, (near_turned,))
    far_expo, far_turned = tall_call(
        place, protos, far_side, 1, STUDENT_SCALE, "tall_expo", student_columns, (col_part,)
    )
    col_half = x_sum(col_part, (far_turned,))
    near_energy, teacher_columns, _ = tall_call(
        place, teacher_protos, near_side, 0, TEACHER_SCALE, "tall_energy", None, (col_half,)
    )
    col_total = ring_sum(col_half, "z")
    row_part = row_call(energy, col_total, total_protos, (near_energy,))
    feat_target = target_call(energy, [made[1] for made in students], col_total, total_protos, (row_part,))
    totals = proto_sum(jnp.concatenate([row_part, soft_part], axis=0))
    mine, other = mix_call(place, feat_target, totals, [made[0] for made in students])
    feat_half = mine + shifted(other, "core", 1)
    (far_energy,) = tall_call(
        place, teacher_protos, far_side, 0, TEACHER_SCALE, "tall_energy", teacher_columns, (totals,)
    )
    grad_part = proto_call(
        place, student_columns, scale_out, [near_energy, far_energy], [near_expo, far_expo], [near_turned, far_turned], col_total,
        ring_parts(totals, "z"), total_protos, (feat_half,),
    )
    pieces = lax.all_to_all(grad_part.reshape(16, width // 16, count // 4), BATCH, 0, 0)
    pieces = pieces.reshape(4, 4, width // 16, count // 4)
    pieces = (pieces[0] + pieces[1]) + (pieces[2] + pieces[3])
    grad_protos = jnp.concatenate([pieces[k] for k in range(4)], axis=1)

    grad_half = finish_call(place, student_feats, ring_parts(feat_half, "y"))
    return join_call(place, grad_half, shifted(grad_half, "core", 1)), grad_protos


def solution(mesh):
    split = Mesh(mesh.devices.reshape(4, 4, 4, 2), ("x", "z", "y", "core"))
    return jax.shard_map(
        on_device,
        mesh=split,
        in_specs=(P(BATCH, None), P(BATCH, None), P(None, PROTO), P(None, PROTO)),
        out_specs=(P(BATCH, None), P(BATCH, PROTO)),
        check_vma=False,
    )
```

```python
import functools

import jax
import jax.numpy as jnp
from jax import lax
from jax.experimental import pallas as pl
from jax.experimental.pallas import tpu as pltpu
from jax.sharding import Mesh
from jax.sharding import PartitionSpec as P

EPSILON = 1e-06
TEACHER_SCALE = 25.0
STUDENT_SCALE = 10.0
LOG2E = 1.4426950408889634
SIZES = {"x": 4, "z": 4, "y": 4, "core": 2}
BATCH = ("x", "z")
PROTO = ("y", "core")
WHOLE = pl.BlockSpec(memory_space=pltpu.VMEM)
SCALARS = pl.BlockSpec(memory_space=pltpu.SMEM)
ANY = pl.BlockSpec(memory_space=pl.ANY)
F32 = jnp.float32
BF16 = jnp.bfloat16


def params(mib):
    return pltpu.CompilerParams(vmem_limit_bytes=mib << 20)


def cost(microseconds):
    return pl.CostEstimate(flops=0, bytes_accessed=int(microseconds * 3.0e6), transcendentals=0)


def in_vmem(value):
    return pltpu.with_memory_space_constraint(value, pltpu.VMEM)


def in_hbm(value):
    return pltpu.with_memory_space_constraint(value, pltpu.HBM)


def unit_rows(values):
    wide = values.astype(F32)
    norms = jnp.sqrt(jnp.sum(wide * wide, axis=1, keepdims=True) + EPSILON)
    return (wide / norms).astype(BF16), norms


def unit_columns(values):
    wide = values.astype(F32)
    norms = jnp.sqrt(jnp.sum(wide * wide, axis=0, keepdims=True) + EPSILON)
    return (wide * (1.0 / norms)).astype(BF16), norms


def across(row, lanes=128):
    return jnp.broadcast_to(row, (lanes, row.shape[1])).T


def two_terms(row):
    high = row.astype(BF16).astype(F32)
    place = lax.broadcasted_iota(jnp.int32, (16, row.shape[1]), 0)
    return jnp.where(place == 0, high, jnp.where(place == 1, row - high, 0.0)).astype(BF16)


def fetch(source, held, arrived, chunk, start=0):
    copies = [
        pltpu.make_async_copy(
            source.at[:, pl.ds(start + at, chunk)], held.at[:, at : at + chunk], arrived.at[at // chunk]
        )
        for at in range(0, held.shape[1], chunk)
    ]
    for copy in copies:
        copy.start()
    return copies


def energy_kernel(place, feats, protos, *refs, size, chunk):
    energy, col_sum, held, arrived = refs[-4:]
    copies = fetch(protos, held, arrived, chunk)
    teacher, _ = unit_rows(feats[...])
    for at in range(0, held.shape[1], size):
        if at % chunk == 0:
            copies[at // chunk].wait()
        unit, _ = unit_columns(held[:, at : at + size])
        score = jnp.dot(teacher, unit, preferred_element_type=F32)
        value = jnp.exp2(score * (TEACHER_SCALE * LOG2E))
        energy[:, at : at + size] = value.astype(BF16)
        col_sum[:, at : at + size] = jnp.sum(value, axis=0, keepdims=True)


def energy_call(place, feats, protos, after=(), size=512, chunk=2048):
    rows, width = feats.shape
    count = protos.shape[1]
    return pl.pallas_call(
        functools.partial(energy_kernel, size=size, chunk=chunk),
        in_specs=[SCALARS, WHOLE, ANY] + [ANY] * len(after),
        out_specs=[WHOLE, WHOLE],
        out_shape=[pltpu.VMEM((rows, count), BF16), jax.ShapeDtypeStruct((1, count), F32)],
        scratch_shapes=[pltpu.VMEM((width, count), BF16), pltpu.SemaphoreType.DMA((count // chunk,))],
        compiler_params=params(10),
        cost_estimate=cost(5.0),
        name="energy",
    )(place, in_hbm(feats), in_hbm(protos), *after)


def units_kernel(place, teacher, student, *refs):
    mine, other = refs[-2:]
    rows, width = mine.shape
    for side, target in ((place[1], mine), (1 - place[1], other)):
        here = pl.ds(pl.multiple_of(side * rows, rows), rows)
        target[:, : width // 2] = unit_rows(teacher[here, :])[0].astype(F32)
        target[:, width // 2 :] = unit_rows(student[here, :])[0].astype(F32)


def units_call(place, teacher, student, after=()):
    rows, width = teacher.shape
    return pl.pallas_call(
        units_kernel,
        in_specs=[SCALARS, WHOLE, WHOLE] + [ANY] * len(after),
        out_specs=[WHOLE] * 2,
        out_shape=[jax.ShapeDtypeStruct((rows // 2, 2 * width), F32)] * 2,
        compiler_params=params(8),
        cost_estimate=cost(1.5),
        name="units",
    )(place, teacher, student, *after)


def add_kernel(first, second, third, fourth, *refs):
    refs[-1][...] = (first[...] + second[...]) + (third[...] + fourth[...])


def add_call(parts, after):
    return pl.pallas_call(
        add_kernel,
        in_specs=[WHOLE] * 4 + [ANY] * len(after),
        out_specs=WHOLE,
        out_shape=jax.ShapeDtypeStruct(parts[0].shape, F32),
        compiler_params=params(4),
        cost_estimate=cost(0.5),
        name="add",
    )(*parts, *after)


def student_kernel(feats, protos, *refs, size, chunk, start):
    feat_part, unit_out, row_sum, held, arrived = refs[-5:]
    copies = fetch(protos, held, arrived, chunk, start)
    student, _ = unit_rows(feats[...])
    total = jnp.zeros((feats.shape[0], 128), F32)
    for at in range(0, held.shape[1], size):
        if at % chunk == 0:
            copies[at // chunk].wait()
        unit, _ = unit_columns(held[:, at : at + size])
        unit_out[:, at : at + size] = unit
        score = jnp.dot(student, unit, preferred_element_type=F32)
        value = jnp.exp2(score * (STUDENT_SCALE * LOG2E))
        part = lax.dot_general(value.astype(BF16), unit, (((1,), (1,)), ((), ())), preferred_element_type=F32)
        feat_part[...] = feat_part[...] + part if at else part
        for tile in range(0, size, 128):
            total = total + value[:, tile : tile + 128]
    row_sum[...] = jnp.sum(total.T, axis=0, keepdims=True)


def student_call(feats, protos, part, parts, after=(), size=512, chunk=2048):
    rows, width = feats.shape
    count = protos.shape[1] // parts
    return pl.pallas_call(
        functools.partial(student_kernel, size=size, chunk=chunk, start=part * count),
        in_specs=[WHOLE, ANY] + [ANY] * len(after),
        out_specs=[WHOLE] * 3,
        out_shape=[
            jax.ShapeDtypeStruct((rows, width), F32),
            pltpu.VMEM((width, count), BF16),
            jax.ShapeDtypeStruct((1, rows), F32),
        ],
        scratch_shapes=[pltpu.VMEM((width, count), BF16), pltpu.SemaphoreType.DMA((count // chunk,))],
        compiler_params=params(10),
        cost_estimate=cost(2.0),
        name="student",
    )(feats, in_hbm(protos), *after)


def tall_kernel(place, protos, *refs, pieces, turn, made, scale, size=512):
    outs = refs[len(refs) - 2 - (1 + turn + 2 * made) : len(refs) - 2]
    energy = outs[0]
    held, arrived = refs[-2:]
    rows = refs[0].shape[0]
    width, count = held.shape
    if made:
        (copy,) = fetch(protos, held, arrived, count, pl.multiple_of(place[0] * count, count))
    side = slice(width, 2 * width) if turn else slice(0, width)
    feats = [refs[k][:, side] for k in range(pieces)]
    if turn:
        for k in range(pieces):
            outs[1][:, k * rows : (k + 1) * rows] = feats[k].T.astype(BF16)
    feats = [value.astype(BF16) for value in feats]
    for at in range(0, count, size):
        here = slice(at, at + size)
        if made:
            if at == 0:
                copy.wait()
            unit, norm = unit_columns(held[:, here])
            outs[-2][:, here] = unit
            outs[-1][:, here] = 1.0 / norm
        else:
            unit = refs[pieces][:, here]
        for k in range(pieces):
            score = jnp.dot(feats[k], unit, preferred_element_type=F32)
            energy[k * rows : (k + 1) * rows, here] = jnp.exp2(score * (scale * LOG2E)).astype(BF16)


def tall_call(place, protos, feats, turn, scale, name, unit=None, after=(), size=512):
    rows = feats[0].shape[0] * len(feats)
    width, count = protos.shape
    count = count // 4
    made = unit is None
    out_shape = [pltpu.VMEM((rows, count), BF16)]
    if turn:
        out_shape.append(jax.ShapeDtypeStruct((width, rows), BF16))
    if made:
        out_shape.append(pltpu.VMEM((width, count), BF16))
        out_shape.append(jax.ShapeDtypeStruct((1, count), F32))
    given = [] if made else [in_vmem(unit)]
    return pl.pallas_call(
        functools.partial(tall_kernel, pieces=len(feats), turn=turn, made=made, scale=scale, size=size),
        in_specs=[SCALARS, ANY] + [WHOLE] * (len(feats) + len(given)) + [ANY] * len(after),
        out_specs=[WHOLE] * len(out_shape),
        out_shape=out_shape,
        scratch_shapes=[pltpu.VMEM((width, count), BF16), pltpu.SemaphoreType.DMA((1,))],
        compiler_params=params(10),
        cost_estimate=cost(2.5),
        name=name,
    )(place, in_hbm(protos), *feats, *given, *after)


def row_kernel(energy, col_total, *refs, total_protos, size=512):
    row_part, lanes, scales = refs[-3:]
    rows, count = energy.shape
    cut = count // 2
    scales[...] = jnp.broadcast_to(1.0 / (total_protos * col_total[:, cut:]), scales.shape)
    total = jnp.zeros((16, rows), F32)
    steps = cut // size
    groups = rows // 16 // steps
    for step in range(steps):
        at = step * size
        scale = two_terms(1.0 / (total_protos * col_total[:, at : at + size]))
        total = total + lax.dot_general(
            scale, energy[:, at : at + size], (((1,), (1,)), ((), ())), preferred_element_type=F32
        )
        for group in range(step * groups, (step + 1) * groups):
            here = slice(group * 16, (group + 1) * 16)
            sums = [jnp.zeros((16, 128), F32)] * 2
            for tile in range((count - cut) // 128):
                lane = slice(tile * 128, (tile + 1) * 128)
                value = energy[here, cut + tile * 128 : cut + (tile + 1) * 128].astype(F32)
                sums[tile % 2] = sums[tile % 2] + value * scales[:, lane]
            lanes[here, :] = sums[0] + sums[1]
    row_part[...] = jnp.sum(total, axis=0, keepdims=True) + jnp.sum(lanes[...].T, axis=0, keepdims=True)


def row_call(energy, col_total, total_protos, after=()):
    rows, count = energy.shape
    return pl.pallas_call(
        functools.partial(row_kernel, total_protos=total_protos),
        in_specs=[WHOLE, WHOLE] + [ANY] * len(after),
        out_specs=WHOLE,
        out_shape=jax.ShapeDtypeStruct((1, rows), F32),
        scratch_shapes=[pltpu.VMEM((rows, 128), F32), pltpu.VMEM((16, count // 2), F32)],
        compiler_params=params(6),
        name="row_pass",
    )(in_vmem(energy), col_total, *after)


def col_kernel(energy, row_total, *refs, total_rows, size=1024):
    col_part = refs[-1]
    scale = two_terms(1.0 / (total_rows * row_total[...]))
    for at in range(0, energy.shape[1], size):
        part = jnp.dot(scale, energy[:, at : at + size], preferred_element_type=F32)
        col_part[:, at : at + size] = jnp.sum(part, axis=0, keepdims=True)


def col_call(energy, row_total, total_rows, after=()):
    return pl.pallas_call(
        functools.partial(col_kernel, total_rows=total_rows),
        in_specs=[WHOLE, WHOLE] + [ANY] * len(after),
        out_specs=WHOLE,
        out_shape=jax.ShapeDtypeStruct((1, energy.shape[1]), F32),
        compiler_params=params(4),
        name="col_pass",
    )(in_vmem(energy), row_total, *after)


def target_kernel(energy, col_total, *refs, parts, total_protos, size):
    unit = refs[:parts]
    feat_part = refs[-1]
    places = [(part, at) for part in unit for at in range(0, part.shape[1], size)]
    for at, (part_of, start) in zip(range(0, energy.shape[1], size), places):
        here = slice(start, start + size)
        scale = 1.0 / (total_protos * col_total[:, at : at + size])
        scaled = (part_of[:, here].astype(F32) * scale).astype(BF16)
        part = lax.dot_general(energy[:, at : at + size], scaled, (((1,), (1,)), ((), ())), preferred_element_type=F32)
        feat_part[...] = feat_part[...] + part if at else part


def target_call(energy, unit, col_total, total_protos, after=(), size=1024):
    parts = len(unit)
    return pl.pallas_call(
        functools.partial(target_kernel, parts=parts, total_protos=total_protos, size=size),
        in_specs=[WHOLE] * (2 + parts) + [ANY] * len(after),
        out_specs=WHOLE,
        out_shape=jax.ShapeDtypeStruct((energy.shape[0], unit[0].shape[0]), F32),
        compiler_params=params(10),
        cost_estimate=cost(3.0),
        name="feat_target",
    )(in_vmem(energy), col_total, *[in_vmem(part) for part in unit], *after)


def mix_kernel(place, target, totals, *refs, parts):
    prob = refs[:parts]
    mine, other, total = refs[-3:]
    wide = target.shape[1] // 128
    rows_r = jnp.concatenate([across(STUDENT_SCALE / totals[:1, :])] * wide, axis=1)
    rows_s = jnp.concatenate([across(STUDENT_SCALE / totals[1:, :])] * wide, axis=1)
    whole = prob[0][...]
    for part in prob[1:]:
        whole = whole + part[...]
    total[...] = whole * rows_s - target[...] * rows_r
    rows = mine.shape[0]
    mine[...] = total[pl.ds(pl.multiple_of(place[1] * rows, rows), rows), :]
    other[...] = total[pl.ds(pl.multiple_of((1 - place[1]) * rows, rows), rows), :]


def mix_call(place, target, totals, prob):
    rows, width = target.shape
    return pl.pallas_call(
        functools.partial(mix_kernel, parts=len(prob)),
        in_specs=[SCALARS] + [WHOLE] * (2 + len(prob)),
        out_specs=[WHOLE] * 2,
        out_shape=[jax.ShapeDtypeStruct((rows // 2, width), F32)] * 2,
        scratch_shapes=[pltpu.VMEM((rows, width), F32)],
        compiler_params=params(10),
        cost_estimate=cost(1.0),
        name="feat_mix",
    )(place, target, totals, *prob)


def proto_kernel(place, unit, scale_out, col_total, *refs, pieces, total_protos, size):
    energy, expo, turned, totals = refs[:2], refs[2:4], refs[4:6], refs[6 : 6 + pieces]
    grad, made, row_scale, soft_scale, left = refs[-5:]
    width, count = unit.shape
    first = pl.multiple_of(place[0] * count, count)
    tall = energy[0].shape[0]
    rows = tall // pieces
    for k in range(pieces):
        for half in range(2):
            side = jnp.where(place[1] == half, 0, 1)
            turn = (pieces - k) % pieces if half else k
            there = pl.ds(pl.multiple_of(side * tall + turn * rows, rows), rows)
            own = STUDENT_SCALE / totals[k][:, half * rows : (half + 1) * rows]
            row_scale[:, there] = own[:1]
            soft_scale[:, there] = own[1:]
    scaled = []
    for side in range(2):
        there = slice(side * tall, (side + 1) * tall)
        wide = turned[side][...].astype(F32)
        scaled.append(((wide * row_scale[:, there]).astype(BF16), (wide * soft_scale[:, there]).astype(BF16)))
    copies = []
    for at in range(0, count, size):
        here = slice(at, at + size)
        scale = 1.0 / (total_protos * col_total[:, pl.ds(first + at, size)])
        target = jnp.dot(scaled[0][0], energy[0][:, here], preferred_element_type=F32)
        target = target + jnp.dot(scaled[1][0], energy[1][:, here], preferred_element_type=F32)
        part = jnp.dot(scaled[0][1], expo[0][:, here], preferred_element_type=F32)
        part = part + jnp.dot(scaled[1][1], expo[1][:, here], preferred_element_type=F32)
        part = part - target * scale
        wide_unit = unit[:, here].astype(F32)
        dots = jnp.sum(wide_unit * part, axis=0, keepdims=True)
        made[:, here] = (part - wide_unit * dots) * scale_out[:, here]
        copies.append(pltpu.make_async_copy(made.at[:, here], grad.at[:, here], left.at[at // size]))
        copies[-1].start()
    for copy in copies:
        copy.wait()


def proto_call(place, unit, scale_out, energy, expo, turned, col_total, totals, total_protos, after=(), size=512):
    rows, count = energy[0].shape
    width = unit.shape[0]
    return pl.pallas_call(
        functools.partial(proto_kernel, pieces=len(totals), total_protos=total_protos, size=size),
        in_specs=[SCALARS] + [WHOLE] * (9 + len(totals)) + [ANY] * len(after),
        out_specs=ANY,
        out_shape=pltpu.HBM((width, count), F32),
        scratch_shapes=[
            pltpu.VMEM((width, count), F32),
            pltpu.VMEM((1, 2 * rows), F32),
            pltpu.VMEM((1, 2 * rows), F32),
            pltpu.SemaphoreType.DMA((count // size,)),
        ],
        compiler_params=params(20),
        cost_estimate=cost(8.0),
        name="proto_grad",
    )(
        place, in_vmem(unit), scale_out, col_total, *[in_vmem(part) for part in energy], *[in_vmem(part) for part in expo],
        *turned, *totals, *after,
    )


def finish_kernel(place, feats, first, second, third, fourth, grad):
    rows = grad.shape[0]
    here = pl.ds(pl.multiple_of(place[1] * rows, rows), rows)
    unit, norm = unit_rows(feats[here, :])
    unit = unit.astype(F32)
    feat_sum = (first[...] + second[...]) + (third[...] + fourth[...])
    along = jnp.sum(unit * feat_sum, axis=1, keepdims=True)
    grad[...] = (feat_sum - unit * along) / norm


def finish_call(place, feats, parts):
    return pl.pallas_call(
        finish_kernel,
        in_specs=[SCALARS] + [WHOLE] * (1 + len(parts)),
        out_specs=WHOLE,
        out_shape=jax.ShapeDtypeStruct(parts[0].shape, F32),
        compiler_params=params(8),
        cost_estimate=cost(1.0),
        name="finish",
    )(place, feats, *parts)


def join_kernel(place, mine, other, whole):
    rows = mine.shape[0]
    whole[pl.ds(pl.multiple_of(place[1] * rows, rows), rows), :] = mine[...]
    whole[pl.ds(pl.multiple_of((1 - place[1]) * rows, rows), rows), :] = other[...]


def join_call(place, mine, other):
    rows, width = mine.shape
    return pl.pallas_call(
        join_kernel,
        in_specs=[SCALARS, WHOLE, WHOLE],
        out_specs=WHOLE,
        out_shape=jax.ShapeDtypeStruct((2 * rows, width), F32),
        compiler_params=params(8),
        cost_estimate=cost(1.0),
        name="join",
    )(place, mine, other)


def shifted(value, axis, shift):
    size = SIZES[axis]
    return lax.ppermute(value, axis, [(i, (i + shift) % size) for i in range(size)])


def two_way(value):
    pairs = []
    for z in range(4):
        pairs.append((2 * z, 2 * ((z + 1) % 4)))
        pairs.append((2 * z + 1, 2 * ((z + 3) % 4) + 1))
    return lax.ppermute(value, ("z", "core"), pairs)


def ring_parts(value, axis):
    made = {shift: shifted(value, axis, shift) for shift in ((1, 3, 2) if SIZES[axis] == 4 else (1,))}
    return [value] + [made[shift] for shift in sorted(made)]


def ring_sum(value, axis):
    parts = ring_parts(value, axis)
    value = parts[0]
    for part in parts[1:]:
        value = value + part
    return value


def batch_sum(value):
    return ring_sum(ring_sum(value, "x"), "z")


def x_sum(value, after):
    return add_call(ring_parts(value, "x"), after)


def proto_sum(value):
    return ring_sum(ring_sum(value, "core"), "y")


def on_device(student_feats, teacher_feats, protos, teacher_protos):
    rows, width = student_feats.shape
    count = protos.shape[1]
    total_rows = rows * 16
    total_protos = count * 8
    place = jnp.stack([lax.axis_index("z"), lax.axis_index("core")]).astype(jnp.int32)

    near, far = units_call(place, teacher_feats, student_feats)
    first = two_way(near)
    energy, col_part = energy_call(place, teacher_feats, teacher_protos)
    col_total = batch_sum(col_part)
    second = two_way(first)
    students = [student_call(student_feats, protos, 0, 2, (col_part,))]
    row_part = row_call(energy, col_total, total_protos, (students[0][2], first))
    students.append(student_call(student_feats, protos, 2, 4, (row_part,)))
    row_total = proto_sum(row_part)
    third = two_way(second)
    col_part = col_call(energy, row_total, total_rows, (second, students[1][2]))
    students.append(student_call(student_feats, protos, 3, 4, (col_part,)))
    soft_part = students[0][2] + students[1][2] + students[2][2]
    col_total = batch_sum(col_part)
    row_part = row_call(energy, col_total, total_protos, (third, students[2][2]))
    near_side = [near, first, second, third]
    far_side = [far] + [shifted(part, "core", 1) for part in (first, second, third)]
    row_total = proto_sum(row_part)
    near_expo, near_turned, student_columns, scale_out = tall_call(
        place, protos, near_side, 1, STUDENT_SCALE, "tall_expo", None, (row_part,)
    )
    col_part = col_call(energy, row_total, total_rows, (near_turned,))
    far_expo, far_turned = tall_call(
        place, protos, far_side, 1, STUDENT_SCALE, "tall_expo", student_columns, (col_part,)
    )
    col_half = x_sum(col_part, (far_turned,))
    near_energy, teacher_columns, _ = tall_call(
        place, teacher_protos, near_side, 0, TEACHER_SCALE, "tall_energy", None, (col_half,)
    )
    col_total = ring_sum(col_half, "z")
    row_part = row_call(energy, col_total, total_protos, (near_energy,))
    feat_target = target_call(energy, [made[1] for made in students], col_total, total_protos, (row_part,))
    totals = proto_sum(jnp.concatenate([row_part, soft_part], axis=0))
    mine, other = mix_call(place, feat_target, totals, [made[0] for made in students])
    feat_half = mine + shifted(other, "core", 1)
    (far_energy,) = tall_call(
        place, teacher_protos, far_side, 0, TEACHER_SCALE, "tall_energy", teacher_columns, (totals,)
    )
    grad_part = proto_call(
        place, student_columns, scale_out, [near_energy, far_energy], [near_expo, far_expo], [near_turned, far_turned], col_total,
        ring_parts(totals, "z"), total_protos, (feat_half,),
    )
    pieces = lax.all_to_all(grad_part.reshape(16, width // 16, count // 4), BATCH, 0, 0)
    pieces = pieces.reshape(4, 4, width // 16, count // 4)
    pieces = (pieces[0] + pieces[1]) + (pieces[2] + pieces[3])
    grad_protos = jnp.concatenate([pieces[k] for k in range(4)], axis=1)

    grad_half = finish_call(place, student_feats, ring_parts(feat_half, "y"))
    return join_call(place, grad_half, shifted(grad_half, "core", 1)), grad_protos


def solution(mesh):
    split = Mesh(mesh.devices.reshape(4, 4, 4, 2), ("x", "z", "y", "core"))
    return jax.shard_map(
        on_device,
        mesh=split,
        in_specs=(P(BATCH, None), P(BATCH, None), P(None, PROTO), P(None, PROTO)),
        out_specs=(P(BATCH, None), P(BATCH, PROTO)),
        check_vma=False,
    )
```
